512 devices in a mesh: group: 16 (over z), ctx: 32 (over x, y, core).
Axes of the slice: x: 4, y: 4, z: 16, core: 2. Of those that a mesh axis runs over, the one named last changes fastest.
Arguments:
- query: bfloat16 [16384, 8192], P('ctx', 'group'), may hold values from -80 to 80
- grad_out: bfloat16 [16384, 8192], P('ctx', 'group'), may hold values from -6 to 6
- key_raw: bfloat16 [1024, 16384], P('group', 'ctx'), may hold values from -4.1 to 4.1
- value_raw: bfloat16 [1024, 16384], P('group', 'ctx'), may hold values from -6 to 6
- beacon_key: bfloat16 [1024, 1024], P('group', 'ctx'), may hold values from -6 to 6
- beacon_value: bfloat16 [1024, 1024], P('group', 'ctx'), may hold values from -6 to 6
- chat_of_span: int32 [32], replicated, may hold values from 0 to 7, never falling along the last dimension, each value on 1 to 17 neighbouring positions
- turn_begin: int32 [16384], P('ctx'), may hold values from 0 to 511, as said below
Outputs:
- grad_query: bfloat16 [16384, 8192], P('ctx', 'group')
- grad_key_raw: float32 [1024, 16384], P('group', 'ctx')
- grad_value_raw: float32 [1024, 16384], P('group', 'ctx')
- grad_beacon_key: float32 [1024, 1024], P('group', 'ctx')
- grad_beacon_value: float32 [1024, 1024], P('group', 'ctx')
The draws below stay inside these ranges and needn't reach their ends.
Inputs may be any that keep to these rules, and one draw needn't show every extreme that they name: `turn_begin`: 0 at a span's first token, never above the token's own position within its span, never falling within a span; a turn begins at the last token of every span.
All inputs are finite; a program needn't handle non-finite values.
Results may differ from the reference program's by a relative error of at most 0.017.
Values may be sent and summed in bfloat16 or wider, within the bound.
A program may use at most 192 MiB of HBM per device.

```python
import math
import jax
import jax.numpy as jnp
import numpy as np
from jax import lax

HD = 128
QH = 64
KVH = 8
SPAN = 512
BPC = 32
NCHUNK = 32
TOKENS = 16384
BEACONS = 1024
N_CTX = 32


def turn_flags(key):
    marks = jax.random.randint(jax.random.fold_in(key, 91), (NCHUNK, SPAN), 0, 48) == 0
    within = jnp.arange(SPAN, dtype=jnp.int32)[None, :]
    firsts = (within == 0) | (within == SPAN - 1)
    return (marks | firsts).reshape(TOKENS)


def base_keys(key):
    return jnp.clip(jax.random.normal(jax.random.fold_in(key, 57), (KVH * HD, TOKENS), jnp.float32), -4.0, 4.0)


def draw_query(key, part):
    key = jax.random.fold_in(key, 3)
    values = jnp.clip(jax.random.normal(key, (TOKENS, QH * HD), jnp.float32), -4.0, 4.0)
    return values.astype(jnp.bfloat16)


def draw_key_raw(key, part):
    keys_base = base_keys(key)
    return keys_base.astype(jnp.bfloat16)


def draw_turn_begin(key, part):
    marks = turn_flags(key).reshape(NCHUNK, SPAN)
    within = jnp.arange(SPAN, dtype=jnp.int32)
    marked = jnp.where(marks, within[None, :], 0)
    return lax.cummax(marked, axis=1).reshape(TOKENS).astype(jnp.int32)


def shard_levels(rng, extent, split, smallest, largest):
    level = 1.0
    for axis_at, blocks in split:
        heights = jax.random.uniform(jax.random.fold_in(jax.random.fold_in(rng, 6), axis_at), (blocks,), jnp.float32, smallest / len(split), largest / len(split))
        level = level * jnp.repeat(jnp.exp(heights), extent[axis_at] // blocks).reshape((-1,) + (1,) * (len(extent) - 1 - axis_at))
    return level


def length_profile(amount, total, bound, skew):
    weights = [(1 << 20) // math.isqrt(standing ** skew) + 1 for standing in range(2, amount + 1)]
    spare, holding = total - bound - (amount - 1), [1] * (amount - 1)
    while spare > 0:
        candidates = [i for i in range(amount - 1) if holding[i] < bound]
        pool, budget = sum([weights[i] for i in candidates]), spare
        for i in candidates:
            extra = min(bound - holding[i], max(1, budget * weights[i] // pool), spare)
            holding[i] = holding[i] + extra
            spare = spare - extra
    return np.array([bound] + holding)


def uneven(stream_key, amount, total, bound, lean):
    if amount == 2:
        one = jax.random.randint(stream_key, (), max(1, total - bound), min(bound, total - 1) + 1)
        return jnp.stack([one, total - one])
    lengths = jnp.asarray(length_profile(amount, total, bound, lean), jnp.int32)
    pairs = (amount - 1) // 2
    donor, receiver = lengths[1:1 + 2 * pairs:2], lengths[2:2 + 2 * pairs:2]
    slack = jnp.minimum(donor - 1, bound - receiver)
    passed = jax.random.randint(jax.random.fold_in(stream_key, 1), (pairs,), 0, 1 << 20) % (slack + 1)
    lengths = lengths.at[1:1 + 2 * pairs:2].set(donor - passed).at[2:2 + 2 * pairs:2].set(receiver + passed)
    return lengths[jax.random.permutation(jax.random.fold_in(stream_key, 2), amount)]


def bell_draw(stream_key, dims, deviation, most, pieces=(), kind=jnp.bfloat16):
    drawn = jax.random.normal(stream_key, dims, jnp.float32) * deviation
    if len(pieces) > 0:
        drawn = shard_levels(stream_key, dims, pieces, -0.22, 0.18) * drawn
    return jnp.clip(drawn, min=-most, max=most).astype(kind)


def setup_inputs(seed: int = 0) -> dict:
    key_of = jax.random.split(jax.random.key(seed), 9)
    query = draw_query(jax.random.fold_in(key_of[8], 71), 0)
    grad_out = bell_draw(key_of[1], (TOKENS, QH * HD), 1.0, 6.0, ((0, 32), (1, 16)))
    key_raw = draw_key_raw(jax.random.fold_in(key_of[8], 71), 0)
    value_raw = bell_draw(key_of[3], (KVH * HD, TOKENS), 1.0, 6.0, ((0, 16), (1, 32)))
    beacon_key = bell_draw(key_of[4], (KVH * HD, BEACONS), 1.0, 6.0, ((0, 16), (1, 32)))
    beacon_value = bell_draw(key_of[5], (KVH * HD, BEACONS), 1.0, 6.0, ((0, 16), (1, 32)))
    chat_of_span = jnp.searchsorted(jnp.cumsum(uneven(key_of[6], N_CTX // 4, NCHUNK, N_CTX // 2 + 1, 1)), jnp.arange(NCHUNK), side="right").astype(jnp.int32)
    turn_begin = draw_turn_begin(jax.random.fold_in(key_of[8], 71), 0)
    return dict(query=query, grad_out=grad_out, key_raw=key_raw, value_raw=value_raw, beacon_key=beacon_key, beacon_value=beacon_value, chat_of_span=chat_of_span, turn_begin=turn_begin)


def reference(query, grad_out, key_raw, value_raw, beacon_key, beacon_value, chat_of_span, turn_begin):
    score_scale = HD ** -0.5
    ratio_heads = QH // KVH
    beacon_total = NCHUNK * BPC
    block_of = jnp.arange(beacon_total, dtype=jnp.int32) // BPC
    local_pos = jnp.arange(SPAN, dtype=jnp.int32)
    chat_of_block = chat_of_span[block_of]

    def one_span(carry, span_index):
        start = (span_index * SPAN).astype(jnp.int32)
        q_rows = lax.dynamic_slice_in_dim(query, start, SPAN, 0)
        d_rows = lax.dynamic_slice_in_dim(grad_out, start, SPAN, 0)
        key_cols = lax.dynamic_slice_in_dim(key_raw, start, SPAN, 1)
        value_cols = lax.dynamic_slice_in_dim(value_raw, start, SPAN, 1)
        begins = lax.dynamic_slice_in_dim(turn_begin, start, SPAN, 0)
        own_chat = chat_of_span[span_index]
        beacon_seen = (block_of < span_index) & (chat_of_block == own_chat)
        raw_seen = (local_pos[None, :] <= local_pos[:, None]) & (local_pos[None, :] >= begins[:, None])
        visible = jnp.concatenate([jnp.broadcast_to(beacon_seen[None, :], (SPAN, beacon_total)), raw_seen], 1)

        def one_group(group_index):
            feature = (group_index * HD).astype(jnp.int32)
            keys_all = jnp.concatenate([lax.dynamic_slice_in_dim(beacon_key, feature, HD, 0),
                                        lax.dynamic_slice_in_dim(key_cols, feature, HD, 0)], 1).astype(jnp.float32)
            values_all = jnp.concatenate([lax.dynamic_slice_in_dim(beacon_value, feature, HD, 0),
                                          lax.dynamic_slice_in_dim(value_cols, feature, HD, 0)], 1).astype(jnp.float32)
            qstart = (group_index * ratio_heads * HD).astype(jnp.int32)
            q_group = lax.dynamic_slice_in_dim(q_rows, qstart, ratio_heads * HD, 1).reshape(SPAN, ratio_heads, HD).astype(jnp.float32)
            d_group = lax.dynamic_slice_in_dim(d_rows, qstart, ratio_heads * HD, 1).reshape(SPAN, ratio_heads, HD).astype(jnp.float32)
            scores = jnp.einsum('thd,dk->htk', q_group, keys_all) * score_scale
            scores = jnp.where(visible[None], scores, -jnp.inf)
            maxima = jnp.max(scores, axis=-1, keepdims=True)
            weights = jnp.exp(scores - maxima)
            probs = weights / jnp.sum(weights, axis=-1, keepdims=True)
            probs_low = lax.optimization_barrier(probs.astype(jnp.bfloat16)).astype(jnp.float32)
            output = jnp.einsum('htk,dk->htd', probs_low, values_all)
            grad_p = jnp.einsum('thd,dk->htk', d_group, values_all)
            row_delta = jnp.sum(jnp.transpose(d_group, (1, 0, 2)) * output, axis=-1, keepdims=True)
            grad_s = lax.optimization_barrier((probs * (grad_p - row_delta)).astype(jnp.bfloat16)).astype(jnp.float32)
            grad_q = (jnp.einsum('htk,dk->thd', grad_s, keys_all) * score_scale).astype(jnp.bfloat16)
            grad_k = jnp.einsum('htk,thd->dk', grad_s, q_group) * score_scale
            grad_v = jnp.einsum('htk,thd->dk', probs_low, d_group)
            return grad_q.reshape(SPAN, ratio_heads * HD), grad_k, grad_v

        grad_q, grad_k, grad_v = lax.map(one_group, jnp.arange(KVH, dtype=jnp.int32))
        grad_q = jnp.transpose(grad_q, (1, 0, 2)).reshape(SPAN, QH * HD)
        grad_k = grad_k.reshape(KVH * HD, beacon_total + SPAN)
        grad_v = grad_v.reshape(KVH * HD, beacon_total + SPAN)
        carry = (carry[0] + grad_k[:, :beacon_total], carry[1] + grad_v[:, :beacon_total])
        return carry, (grad_q, grad_k[:, beacon_total:], grad_v[:, beacon_total:])

    zeros = jnp.zeros((KVH * HD, beacon_total), jnp.float32)
    sums, stacked = lax.scan(one_span, (zeros, zeros), jnp.arange(NCHUNK, dtype=jnp.int32))
    grad_query = stacked[0].reshape(TOKENS, QH * HD)
    grad_key_raw = jnp.transpose(stacked[1], (1, 0, 2)).reshape(KVH * HD, TOKENS)
    grad_value_raw = jnp.transpose(stacked[2], (1, 0, 2)).reshape(KVH * HD, TOKENS)
    return grad_query, grad_key_raw, grad_value_raw, sums[0], sums[1]
```

```python
import functools
import math

import jax
import jax.numpy as jnp
from jax import lax
from jax.experimental import pallas as pl
from jax.experimental.pallas import tpu as pltpu
from jax.sharding import PartitionSpec as P

MESH = pl.DeviceIdType.MESH
F32 = jnp.float32
BF16 = jnp.bfloat16
HIDDEN = -1e30
BLOCK = 128


def dot(a, b):
    return lax.dot_general(a, b, (((1,), (0,)), ((), ())), preferred_element_type=F32)


def kernel(
    n_ctx,
    window,
    chat_ref,
    q_hbm,
    do_hbm,
    k_hbm,
    v_hbm,
    bk_hbm,
    bv_hbm,
    turn_hbm,
    gq_ref,
    gk_ref,
    gv_ref,
    gbk_ref,
    gbv_ref,
    q,
    do,
    khalf,
    vhalf,
    bkhalf,
    bvhalf,
    turn,
    qt,
    dot_t,
    bias,
    kfull,
    vfull,
    kt,
    vt,
    beacon_out,
    beacon_in,
    mine,
    bkv,
    bkey,
    e_raw,
    e_b,
    dp_raw,
    dp_b,
    p_raw,
    p_b,
    s_raw,
    s_b,
    stats,
    gkt,
    gvt,
    gout,
    gin,
    gb_out,
    gb_in,
    gp_out,
    gp_in,
    load_sem,
    pair_send,
    pair_recv,
    b_send,
    b_recv,
    g_send,
    g_recv,
):
    heads = qt.shape[0]
    span = q.shape[0]
    per = bk_hbm.shape[1]
    half = khalf.shape[0]
    width = 2 * half
    nb = window * per
    blocks = span // BLOCK
    scale = width ** (-0.5)
    factor = scale * math.log2(math.e)

    z = lax.axis_index("group")
    me = lax.axis_index("ctx")
    parity = lax.rem(z, 2)
    partner = z + 1 - 2 * parity

    loads = [
        pltpu.make_async_copy(src, dst, load_sem.at[i])
        for i, (src, dst) in enumerate(
            (
                (bk_hbm, bkhalf),
                (bv_hbm, bvhalf),
                (k_hbm, khalf),
                (v_hbm, vhalf),
                (q_hbm, q),
                (do_hbm, do),
                (turn_hbm, turn),
            )
        )
    ]
    for copy in loads:
        copy.start()

    barrier = pltpu.get_barrier_semaphore()
    pl.semaphore_signal(barrier, inc=1, device_id=(partner, me), device_id_type=MESH)

    def greet(i, carry):
        other = lax.rem(me + i, n_ctx)
        pl.semaphore_signal(barrier, inc=1, device_id=(z, other), device_id_type=MESH)
        return carry

    lax.fori_loop(1, n_ctx, greet, 0)

    loads[0].wait()
    loads[1].wait()
    small = jnp.concatenate(
        [bkhalf[...].astype(F32).T, bvhalf[...].astype(F32).T], axis=1
    )
    beacon_out[...] = small.astype(BF16)
    loads[2].wait()
    loads[3].wait()
    pl.semaphore_wait(barrier, n_ctx)

    def to_partner(i, src, dst):
        return pltpu.make_async_remote_copy(
            src_ref=src,
            dst_ref=dst,
            send_sem=pair_send.at[i],
            recv_sem=pair_recv.at[i],
            device_id=(partner, me),
            device_id_type=MESH,
        )

    pair = [
        to_partner(0, beacon_out, beacon_in),
        to_partner(1, khalf, kfull.at[pl.ds(parity * half, half)]),
        to_partner(2, vhalf, vfull.at[pl.ds(parity * half, half)]),
    ]
    for copy in pair:
        copy.start()

    kfull[pl.ds(parity * half, half), :] = khalf[...]
    vfull[pl.ds(parity * half, half), :] = vhalf[...]

    loads[4].wait()
    loads[5].wait()
    loads[6].wait()
    for h in range(heads):
        qt[h] = q[:, h * width : (h + 1) * width].T
        dot_t[h] = do[:, h * width : (h + 1) * width].T
    begin = turn[...].reshape(1, span)
    rows = lax.broadcasted_iota(jnp.int32, (BLOCK, span), 0)
    cols = lax.broadcasted_iota(jnp.int32, (BLOCK, span), 1)
    for b in range(blocks):
        at = rows + b * BLOCK
        seen = (at <= cols) & (at >= begin)
        bias[b * BLOCK : (b + 1) * BLOCK, :] = jnp.where(seen, 0.0, HIDDEN)

    pair[0].wait_recv()
    own = beacon_out[...]
    other = beacon_in[...]
    low = jnp.where(parity == 0, own, other)
    high = jnp.where(parity == 0, other, own)
    mine[...] = jnp.concatenate(
        [low[:, :half], high[:, :half], low[:, half:], high[:, half:]], axis=1
    )

    def push(i, carry):
        pltpu.make_async_remote_copy(
            src_ref=mine,
            dst_ref=bkv.at[pl.ds(i * per, per)],
            send_sem=b_send,
            recv_sem=b_recv,
            device_id=(z, lax.rem(me + 1 + i, n_ctx)),
            device_id_type=MESH,
        ).start()
        return carry

    lax.fori_loop(0, window, push, 0)

    pair[1].wait_recv()
    kt[...] = kfull[...].T
    pair[2].wait_recv()
    vt[...] = vfull[...].T

    def raw(h, carry):
        top = None
        for b in range(blocks):
            lo, hi = b * BLOCK, (b + 1) * BLOCK
            s = dot(kt[lo:hi, :], qt[h, :, lo:]) * factor + bias[lo:hi, lo:]
            e_raw[h, lo:hi, lo:] = s
            m = jnp.max(s, axis=0, keepdims=True)
            if lo:
                m = jnp.concatenate([jnp.full((1, lo), HIDDEN, F32), m], axis=1)
            top = m if top is None else jnp.maximum(top, m)
        total = jnp.zeros((1, span), F32)
        delta = jnp.zeros((1, span), F32)
        for b in range(blocks):
            lo, hi = b * BLOCK, (b + 1) * BLOCK
            e = jnp.exp2(e_raw[h, lo:hi, lo:] - top[:, lo:])
            e_raw[h, lo:hi, lo:] = e
            g = dot(vt[lo:hi, :], dot_t[h, :, lo:])
            dp_raw[h, lo:hi, lo:] = g
            t = jnp.sum(e, axis=0, keepdims=True)
            d = jnp.sum(e * g, axis=0, keepdims=True)
            if lo:
                zeros = jnp.zeros((1, lo), F32)
                t = jnp.concatenate([zeros, t], axis=1)
                d = jnp.concatenate([zeros, d], axis=1)
            total = total + t
            delta = delta + d
        stats[h, 0:1, :] = top
        stats[h, 1:2, :] = total
        stats[h, 2:3, :] = delta
        return carry

    lax.fori_loop(0, heads, raw, 0)

    pltpu.make_async_copy(bkv, bkv, b_recv).wait()
    bkey[...] = bkv[:, :width].T

    chat = chat_ref[me]

    def beacons(h, carry):
        top_raw = stats[h, 0:1, :]
        top = top_raw
        for i in range(window):
            lo, hi = i * per, (i + 1) * per
            span_id = me - 1 - i
            shown = (span_id >= 0) & (chat_ref[jnp.maximum(span_id, 0)] == chat)
            shift = jnp.where(shown, 0.0, HIDDEN).astype(F32)
            s = dot(bkv[lo:hi, :width], qt[h]) * factor + shift
            e_b[h, lo:hi, :] = s
            top = jnp.maximum(top, jnp.max(s, axis=0, keepdims=True))
        total = jnp.zeros((1, span), F32)
        delta = jnp.zeros((1, span), F32)
        for lo in range(0, nb, 64):
            hi = min(lo + 64, nb)
            e = jnp.exp2(e_b[h, lo:hi, :] - top)
            e_b[h, lo:hi, :] = e
            g = dot(bkv[lo:hi, width:], dot_t[h])
            dp_b[h, lo:hi, :] = g
            total = total + jnp.sum(e, axis=0, keepdims=True)
            delta = delta + jnp.sum(e * g, axis=0, keepdims=True)
        alpha = jnp.exp2(top_raw - top)
        inv = 1.0 / (total + alpha * stats[h, 1:2, :])
        f_raw = alpha * inv
        delta = delta * inv + f_raw * stats[h, 2:3, :]
        for lo in range(0, nb, 64):
            hi = min(lo + 64, nb)
            p = e_b[h, lo:hi, :] * inv
            p_b[h, lo:hi, :] = p.astype(BF16)
            s_b[h, lo:hi, :] = (p * (dp_b[h, lo:hi, :] - delta)).astype(BF16)
        for b in range(blocks):
            lo, hi = b * BLOCK, (b + 1) * BLOCK
            p = e_raw[h, lo:hi, lo:] * f_raw[:, lo:]
            p_raw[h, lo:hi, lo:] = p.astype(BF16)
            s_raw[h, lo:hi, lo:] = (p * (dp_raw[h, lo:hi, lo:] - delta[:, lo:])).astype(BF16)
            if b % 2:
                s_raw[h, lo:hi, lo - BLOCK : lo] = jnp.zeros((BLOCK, BLOCK), BF16)
        return carry

    lax.fori_loop(0, heads, beacons, 0)

    gk_b = jnp.zeros((nb, width), F32)
    gv_b = jnp.zeros((nb, width), F32)
    for h in range(heads):
        gk_b = gk_b + dot(s_b[h], q[:, h * width : (h + 1) * width])
        gv_b = gv_b + dot(p_b[h], do[:, h * width : (h + 1) * width])
    gb_out[:, :width] = (gk_b * scale).astype(BF16)
    gb_out[:, width:] = gv_b.astype(BF16)

    def push_back(i, carry):
        pltpu.make_async_remote_copy(
            src_ref=gb_out.at[pl.ds(i * per, per)],
            dst_ref=gb_in.at[pl.ds(i * per, per)],
            send_sem=g_send,
            recv_sem=g_recv,
            device_id=(z, lax.rem(me + n_ctx - 1 - i, n_ctx)),
            device_id_type=MESH,
        ).start()
        return carry

    lax.fori_loop(0, window, push_back, 0)

    for b in range(blocks):
        lo, hi = b * BLOCK, (b + 1) * BLOCK
        gk = jnp.zeros((BLOCK, width), F32)
        gv = jnp.zeros((BLOCK, width), F32)
        for h in range(heads):
            gk = gk + dot(s_raw[h, lo:hi, lo:], q[lo:, h * width : (h + 1) * width])
            gv = gv + dot(p_raw[h, lo:hi, lo:], do[lo:, h * width : (h + 1) * width])
        gkt[:, lo:hi] = (gk * scale).T
        gvt[:, lo:hi] = gv.T

    mine_at = pl.ds(parity * half, half)
    theirs_at = pl.ds((1 - parity) * half, half)
    gout[0] = gkt[theirs_at, :].astype(BF16)
    gout[1] = gvt[theirs_at, :].astype(BF16)
    pair_g = to_partner(3, gout, gin)
    pair_g.start()

    step = 2 * BLOCK

    def queries(h, carry):
        for lo in range(0, span, step):
            hi = lo + step
            g = dot(kfull[:, :hi], s_raw[h, :hi, lo:hi]) + dot(bkey[...], s_b[h, :, lo:hi])
            gq_ref[lo:hi, pl.ds(h * width, width)] = (g * scale).T.astype(BF16)
        return carry

    for h in range(heads):
        queries(h, 0)

    pltpu.make_async_copy(gb_in, gb_in, g_recv).wait()
    gsum = jnp.zeros((per, 2 * width), F32)
    for i in range(window):
        gsum = gsum + gb_in[i * per : (i + 1) * per, :].astype(F32)
    low = jnp.concatenate([gsum[:, :half], gsum[:, width : width + half]], axis=1)
    high = jnp.concatenate([gsum[:, half:width], gsum[:, width + half :]], axis=1)
    gp_out[...] = jnp.where(parity == 0, high, low).astype(BF16)
    pair_b = to_partner(4, gp_out, gp_in)
    pair_b.start()
    kept = jnp.where(parity == 0, low, high)

    pair_g.wait_recv()
    gk_ref[...] = gkt[mine_at, :] + gin[0].astype(F32)
    gv_ref[...] = gvt[mine_at, :] + gin[1].astype(F32)

    pair_b.wait_recv()
    final = kept + gp_in[...].astype(F32)
    gbk_ref[...] = final[:, :half].T
    gbv_ref[...] = final[:, half:].T

    for copy in pair:
        copy.wait_send()
    pair_g.wait_send()
    pair_b.wait_send()
    pltpu.make_async_copy(bkv, bkv, b_send).wait()
    pltpu.make_async_copy(gb_out, gb_out, g_send).wait()


def on_device(
    n_ctx, query, grad_out, key_raw, value_raw, beacon_key, beacon_value, chat_of_span, turn_begin
):
    span, lanes = query.shape
    half, per = beacon_key.shape
    width = 2 * half
    heads = lanes // width
    window = min(16, n_ctx - 1)
    nb = window * per
    vmem = pltpu.VMEM
    anywhere = pl.BlockSpec(memory_space=pl.ANY)
    dma = pltpu.SemaphoreType.DMA
    return pl.pallas_call(
        functools.partial(kernel, n_ctx, window),
        out_shape=(
            jax.ShapeDtypeStruct((span, lanes), BF16),
            jax.ShapeDtypeStruct((half, span), F32),
            jax.ShapeDtypeStruct((half, span), F32),
            jax.ShapeDtypeStruct((half, per), F32),
            jax.ShapeDtypeStruct((half, per), F32),
        ),
        in_specs=[pl.BlockSpec(memory_space=pltpu.SMEM)] + [anywhere] * 7,
        out_specs=[pl.BlockSpec(memory_space=pltpu.VMEM)] * 5,
        scratch_shapes=[
            vmem((span, lanes), BF16),
            vmem((span, lanes), BF16),
            vmem((half, span), BF16),
            vmem((half, span), BF16),
            vmem((half, per), BF16),
            vmem((half, per), BF16),
            vmem((span,), jnp.int32),
            vmem((heads, width, span), BF16),
            vmem((heads, width, span), BF16),
            vmem((span, span), F32),
            vmem((width, span), BF16),
            vmem((width, span), BF16),
            vmem((span, width), BF16),
            vmem((span, width), BF16),
            vmem((per, width), BF16),
            vmem((per, width), BF16),
            vmem((per, 2 * width), BF16),
            vmem((nb, 2 * width), BF16),
            vmem((width, nb), BF16),
            vmem((heads, span, span), F32),
            vmem((heads, nb, span), F32),
            vmem((heads, span, span), F32),
            vmem((heads, nb, span), F32),
            vmem((heads, span, span), BF16),
            vmem((heads, nb, span), BF16),
            vmem((heads, span, span), BF16),
            vmem((heads, nb, span), BF16),
            vmem((heads, 8, span), F32),
            vmem((width, span), F32),
            vmem((width, span), F32),
            vmem((2, half, span), BF16),
            vmem((2, half, span), BF16),
            vmem((nb, 2 * width), BF16),
            vmem((nb, 2 * width), BF16),
            vmem((per, width), BF16),
            vmem((per, width), BF16),
            dma((7,)),
            dma((5,)),
            dma((5,)),
            dma,
            dma,
            dma,
            dma,
        ],
        compiler_params=pltpu.CompilerParams(
            collective_id=0, has_side_effects=True, vmem_limit_bytes=48 * 1024 * 1024
        ),
        cost_estimate=pl.CostEstimate(
            flops=10 * heads * span * (span + nb) * width,
            bytes_accessed=6 * span * lanes,
            transcendentals=heads * span * (span + nb),
        ),
        name="beacon_backward",
    )(chat_of_span, query, grad_out, key_raw, value_raw, beacon_key, beacon_value, turn_begin)


def solution(mesh):
    in_specs = (
        P("ctx", "group"),
        P("ctx", "group"),
        P("group", "ctx"),
        P("group", "ctx"),
        P("group", "ctx"),
        P("group", "ctx"),
        P(),
        P("ctx"),
    )
    out_specs = (
        P("ctx", "group"),
        P("group", "ctx"),
        P("group", "ctx"),
        P("group", "ctx"),
        P("group", "ctx"),
    )
    return jax.shard_map(
        functools.partial(on_device, mesh.shape["ctx"]),
        mesh=mesh,
        in_specs=in_specs,
        out_specs=out_specs,
        check_vma=False,
    )
```

```python
import functools
import math
import types

import jax
import jax.numpy as jnp
from jax import lax
from jax.experimental import pallas as pl
from jax.experimental.pallas import tpu as pltpu
from jax.sharding import PartitionSpec as P

MESH = pl.DeviceIdType.MESH
F32 = jnp.float32
BF16 = jnp.bfloat16
HIDDEN = -1e30
BLOCK = 128
LOG2E = math.log2(math.e)


def dot(a, b):
    return lax.dot_general(a, b, (((1,), (0,)), ((), ())), preferred_element_type=F32)


def head_lanes(h, width):
    return slice(h * width, (h + 1) * width)


def turn_queries(r, d):
    for h in range(d.heads):
        r.qt[h] = r.q[:, head_lanes(h, d.width)].T
        r.dot_t[h] = r.do[:, head_lanes(h, d.width)].T


def hide_tokens(r, d):
    begin = r.turn[...].reshape(1, d.span)
    rows = lax.broadcasted_iota(jnp.int32, (BLOCK, d.span), 0)
    cols = lax.broadcasted_iota(jnp.int32, (BLOCK, d.span), 1)
    for lo in range(0, d.span, BLOCK):
        at = rows + lo
        seen = (at <= cols) & (at >= begin)
        r.bias[lo : lo + BLOCK, :] = jnp.where(seen, 0.0, HIDDEN)


def widen(row, lo, fill):
    if lo == 0:
        return row
    return jnp.concatenate([jnp.full((1, lo), fill, F32), row], axis=1)


def raw_part(r, d, h):
    top = jnp.full((1, d.span), HIDDEN, F32)
    for lo in range(0, d.span, BLOCK):
        hi = lo + BLOCK
        s = dot(r.kt[lo:hi, :], r.qt[h, :, lo:]) * d.factor + r.bias[lo:hi, lo:]
        r.e_raw[h, lo:hi, lo:] = s
        top = jnp.maximum(top, widen(jnp.max(s, axis=0, keepdims=True), lo, HIDDEN))
    total = jnp.zeros((1, d.span), F32)
    delta = jnp.zeros((1, d.span), F32)
    for lo in range(0, d.span, BLOCK):
        hi = lo + BLOCK
        e = jnp.exp2(r.e_raw[h, lo:hi, lo:] - top[:, lo:])
        r.e_raw[h, lo:hi, lo:] = e
        g = dot(r.vt[lo:hi, :], r.dot_t[h, :, lo:])
        r.dp_raw[h, lo:hi, lo:] = g
        total = total + widen(jnp.sum(e, axis=0, keepdims=True), lo, 0.0)
        delta = delta + widen(jnp.sum(e * g, axis=0, keepdims=True), lo, 0.0)
    r.stats[h, 0:1, :] = top
    r.stats[h, 1:2, :] = total
    r.stats[h, 2:3, :] = delta


def blocks_of(d, part):
    base = part * d.nb
    return [(lo, min(lo + BLOCK, base + d.nb)) for lo in range(base, base + d.nb, BLOCK)]


def slot_shifts(r, d, me, part):
    core = lax.rem(me, 2)
    chat = r.chat[me]
    shifts = []
    for k in range(1, d.window + 1):
        if part == 0:
            span_id = me - 2 * k
        elif k < d.window:
            span_id = me + 1 - 2 * core - 2 * k
        else:
            span_id = me - core + (1 - core) * (1 - 2 * k)
        shown = (span_id >= 0) & (r.chat[jnp.maximum(span_id, 0)] == chat)
        shifts.append(jnp.where(shown, 0.0, HIDDEN).astype(F32))
    return shifts


def beacon_part(r, d, h, part, shifts):
    top = jnp.full((1, d.span), HIDDEN, F32)
    for lo, hi in blocks_of(d, part):
        s = dot(r.bkv[lo:hi, : d.width], r.qt[h]) * d.factor
        for at in range(lo, hi, d.per):
            moved = s[at - lo : at - lo + d.per] + shifts[(at - part * d.nb) // d.per]
            r.e_b[h, at : at + d.per, :] = moved
            top = jnp.maximum(top, jnp.max(moved, axis=0, keepdims=True))
    total = jnp.zeros((1, d.span), F32)
    delta = jnp.zeros((1, d.span), F32)
    for lo, hi in blocks_of(d, part):
        e = jnp.exp2(r.e_b[h, lo:hi, :] - top)
        r.e_b[h, lo:hi, :] = e
        g = dot(r.bkv[lo:hi, d.width :], r.dot_t[h])
        r.dp_b[h, lo:hi, :] = g
        total = total + jnp.sum(e, axis=0, keepdims=True)
        delta = delta + jnp.sum(e * g, axis=0, keepdims=True)
    at = 3 * (part + 1)
    r.stats[h, at : at + 1, :] = top
    r.stats[h, at + 1 : at + 2, :] = total
    r.stats[h, at + 2 : at + 3, :] = delta


def combine(r, d, h):
    tops = [r.stats[h, i : i + 1, :] for i in (0, 3, 6)]
    top = jnp.maximum(jnp.maximum(tops[0], tops[1]), tops[2])
    factors = [jnp.exp2(t - top) for t in tops]
    total = jnp.zeros((1, d.span), F32)
    delta = jnp.zeros((1, d.span), F32)
    for i, f in enumerate(factors):
        total = total + f * r.stats[h, 3 * i + 1 : 3 * i + 2, :]
        delta = delta + f * r.stats[h, 3 * i + 2 : 3 * i + 3, :]
    inv = 1.0 / total
    for i, f in enumerate(factors):
        r.stats[h, 9 + i : 10 + i, :] = f * inv
    r.stats[h, 12:13, :] = delta * inv


def beacon_probs(r, d, h, part):
    f = r.stats[h, 10 + part : 11 + part, :]
    delta = r.stats[h, 12:13, :]
    for lo, hi in blocks_of(d, part):
        p = r.e_b[h, lo:hi, :] * f
        r.p_b[h, lo:hi, :] = p.astype(BF16)
        r.s_b[h, lo:hi, :] = (p * (r.dp_b[h, lo:hi, :] - delta)).astype(BF16)


def raw_probs(r, d, h):
    f = r.stats[h, 9:10, :]
    delta = r.stats[h, 12:13, :]
    for lo in range(0, d.span, BLOCK):
        hi = lo + BLOCK
        p = r.e_raw[h, lo:hi, lo:] * f[:, lo:]
        r.p_raw[h, lo:hi, lo:] = p.astype(BF16)
        r.s_raw[h, lo:hi, lo:] = (p * (r.dp_raw[h, lo:hi, lo:] - delta[:, lo:])).astype(BF16)
        if lo % (2 * BLOCK):
            r.s_raw[h, lo:hi, lo - BLOCK : lo] = jnp.zeros((BLOCK, BLOCK), BF16)


def beacon_grads(r, d, part):
    at = slice(part * d.nb, (part + 1) * d.nb)
    gk = jnp.zeros((d.nb, d.width), F32)
    gv = jnp.zeros((d.nb, d.width), F32)
    for h in range(d.heads):
        gk = gk + dot(r.s_b[h, at, :], r.q[:, head_lanes(h, d.width)])
        gv = gv + dot(r.p_b[h, at, :], r.do[:, head_lanes(h, d.width)])
    return gk * d.scale, gv


def grads_to_sibling(r, d):
    gk, gv = beacon_grads(r, d, 1)
    r.x_out[:, : d.width] = gk.astype(BF16)
    r.x_out[:, d.width :] = gv.astype(BF16)


def pack_halves(ref, at, gk, gv, half):
    ref[0, at, :] = jnp.concatenate([gk[:, :half], gv[:, :half]], axis=1).astype(BF16)
    ref[1, at, :] = jnp.concatenate([gk[:, half:], gv[:, half:]], axis=1).astype(BF16)


def raw_key_grads(r, d, lhs, rhs, out, scale):
    for lo in range(0, d.span, BLOCK):
        hi = lo + BLOCK
        g = jnp.zeros((BLOCK, d.width), F32)
        for h in range(d.heads):
            g = g + dot(lhs[h, lo:hi, lo:], rhs[lo:, head_lanes(h, d.width)])
        out[:, lo:hi] = (g * scale).T


def query_grads(r, d, h):
    for lo in range(0, d.span, 2 * BLOCK):
        hi = lo + 2 * BLOCK
        g = dot(r.kfull[:, :hi], r.s_raw[h, :hi, lo:hi]) + dot(r.bkey[...], r.s_b[h, :, lo:hi])
        r.gq[lo:hi, head_lanes(h, d.width)] = (g * d.scale).T.astype(BF16)


def unfold(r, d, part, halves):
    low, high = halves[0], halves[1]
    half = d.half
    r.bkv[part * d.nb : (part + 1) * d.nb, :] = jnp.concatenate(
        [low[:, :half], high[:, :half], low[:, half:], high[:, half:]], axis=1
    )


def each_head(d, step):
    def one(h, carry):
        step(h)
        return carry

    lax.fori_loop(0, d.heads, one, 0)


def wait_for(ref, sem):
    pltpu.make_async_copy(ref, ref, sem).wait()


def kernel(names, d, *refs):
    r = types.SimpleNamespace(**dict(zip(names, refs)))
    per, half, window, n_ctx = d.per, d.half, d.window, d.n_ctx

    z = lax.axis_index("group")
    me = lax.axis_index("ctx")
    parity = lax.rem(z, 2)
    even = z - parity
    partner = z + 1 - 2 * parity
    core = lax.rem(me, 2)
    sibling = me + 1 - 2 * core
    my_rows = pl.ds(parity * half, half)
    their_rows = pl.ds((1 - parity) * half, half)
    shared = pl.ds(0, (window - 1) * per)
    last = pl.ds((window - 1) * per, per)
    beyond = pl.ds(window * per, per)

    loads = [
        pltpu.make_async_copy(src, dst, r.load_sem.at[i])
        for i, (src, dst) in enumerate(
            (
                (r.bk_hbm, r.bkhalf),
                (r.bv_hbm, r.bvhalf),
                (r.k_hbm, r.kfull.at[my_rows]),
                (r.v_hbm, r.vfull.at[my_rows]),
                (r.q_hbm, r.q),
                (r.do_hbm, r.do),
                (r.turn_hbm, r.turn),
                (r.chat_hbm, r.chat),
            )
        )
    ]
    for copy in loads:
        copy.start()

    barrier = pltpu.get_barrier_semaphore()

    def greet(group, ctx):
        pl.semaphore_signal(barrier, inc=1, device_id=(group, ctx), device_id_type=MESH)

    def greet_earlier(i, carry):
        k = window - i // 2
        greet(even + lax.rem(i, 2), lax.rem(me + n_ctx - 2 * k, n_ctx))
        return carry

    lax.fori_loop(0, 2 * window, greet_earlier, 0)
    greet(partner, me)
    greet(z, sibling)
    greet(partner, sibling)

    loads[0].wait()
    loads[1].wait()
    r.beacon_out[...] = jnp.concatenate([r.bkhalf[...], r.bvhalf[...]], axis=1)
    loads[2].wait()
    loads[3].wait()
    pl.semaphore_wait(barrier, 2 * window + 3)

    def remote(src, dst, send, recv, group, ctx):
        return pltpu.make_async_remote_copy(
            src_ref=src,
            dst_ref=dst,
            send_sem=send,
            recv_sem=recv,
            device_id=(group, ctx),
            device_id_type=MESH,
        )

    def to_partner(i, src, dst):
        return remote(src, dst, r.pair_send.at[i], r.pair_recv.at[i], partner, me)

    def to_sibling(i, src, dst):
        return remote(src, dst, r.core_send.at[i], r.core_recv.at[i], z, sibling)

    pair = [
        to_partner(0, r.kfull.at[my_rows], r.kfull.at[my_rows]),
        to_partner(1, r.vfull.at[my_rows], r.vfull.at[my_rows]),
        to_partner(2, r.gout.at[0], r.gin.at[0]),
        to_partner(3, r.gout.at[1], r.gin.at[1]),
    ]
    cores = [
        to_sibling(0, r.b_in.at[:, shared], r.b_sib.at[:, shared]),
        to_sibling(1, r.b_in.at[:, last], r.b_sib.at[:, last]),
        to_sibling(2, r.x_out.at[shared], r.x_in.at[shared]),
        to_sibling(3, r.x_out.at[last], r.x_in.at[last]),
    ]

    pair[0].start()

    def push(i, carry):
        k = window - i // 2
        remote(
            r.beacon_out,
            r.b_in.at[parity, pl.ds((k - 1) * per, per)],
            r.b_send,
            r.b_recv,
            even + lax.rem(i, 2),
            lax.rem(me + 2 * k, n_ctx),
        ).start()
        return carry

    lax.fori_loop(0, 2 * window, push, 0)
    pair[1].start()

    own_chip = [
        remote(
            r.beacon_out,
            r.b_sib.at[parity, last],
            r.own_send.at[i],
            r.own_recv,
            group,
            sibling,
        )
        for i, group in enumerate((z, partner))
    ]

    @pl.when(core == 0)
    def _():
        for copy in own_chip:
            copy.start()

    for i in (4, 5, 6, 7):
        loads[i].wait()
    turn_queries(r, d)
    hide_tokens(r, d)

    @pl.when(core == 0)
    def _():
        r.x_in[last, :] = jnp.zeros((per, 2 * d.width), BF16)

    @pl.when(core == 1)
    def _():
        r.red[:, beyond, :] = jnp.zeros((2, per, d.width), BF16)

    wait_for(r.b_in, r.b_recv)
    cores[0].start()

    @pl.when(core == 1)
    def _():
        cores[1].start()

    pair[0].wait_recv()
    r.kt[...] = r.kfull[...].T
    pair[1].wait_recv()
    r.vt[...] = r.vfull[...].T
    each_head(d, lambda h: raw_part(r, d, h))

    unfold(r, d, 0, r.b_in)
    shifts = slot_shifts(r, d, me, 0)
    each_head(d, lambda h: beacon_part(r, d, h, 0, shifts))

    cores[0].wait_recv()

    @pl.when(core == 0)
    def _():
        cores[1].wait_recv()

    @pl.when(core == 1)
    def _():
        wait_for(r.b_sib.at[:, last], r.own_recv)

    unfold(r, d, 1, r.b_sib)
    shifts_sib = slot_shifts(r, d, me, 1)

    def second(h):
        beacon_part(r, d, h, 1, shifts_sib)
        combine(r, d, h)
        beacon_probs(r, d, h, 1)

    each_head(d, second)
    grads_to_sibling(r, d)
    cores[2].start()

    @pl.when(core == 0)
    def _():
        cores[3].start()

    tail = r.x_out[last, :]
    pack_halves(r.own_out, slice(None), tail[:, : d.width], tail[:, d.width :], half)
    own_back = [
        remote(
            r.own_out.at[p],
            r.red.at[parity, beyond],
            r.back_send.at[p],
            r.back_recv,
            even + p,
            sibling,
        )
        for p in range(2)
    ]

    @pl.when(core == 1)
    def _():
        for copy in own_back:
            copy.start()

    each_head(d, lambda h: beacon_probs(r, d, h, 0))
    gk, gv = beacon_grads(r, d, 0)
    cores[2].wait_recv()

    @pl.when(core == 1)
    def _():
        cores[3].wait_recv()

    gk = gk + r.x_in[:, : d.width].astype(F32)
    gv = gv + r.x_in[:, d.width :].astype(F32)
    pack_halves(r.g_out, slice(None), gk, gv, half)

    def push_back(i, carry):
        k = window - i // 2
        p = lax.rem(i, 2)
        at = pl.ds((k - 1) * per, per)
        remote(
            r.g_out.at[p, at],
            r.red.at[parity, at],
            r.g_send,
            r.g_recv,
            even + p,
            lax.rem(me + n_ctx - 2 * k, n_ctx),
        ).start()
        return carry

    lax.fori_loop(0, 2 * window, push_back, 0)

    each_head(d, lambda h: raw_probs(r, d, h))
    raw_key_grads(r, d, r.p_raw, r.do, r.gvt, 1.0)
    r.gout[1] = r.gvt[their_rows, :].astype(BF16)
    pair[3].start()
    raw_key_grads(r, d, r.s_raw, r.q, r.gkt, d.scale)
    r.gout[0] = r.gkt[their_rows, :].astype(BF16)
    pair[2].start()

    r.bkey[...] = r.bkv[:, : d.width].T
    for h in range(d.heads):
        query_grads(r, d, h)

    whole = pl.ds(0, window * per)
    wait_for(r.red.at[:, whole], r.g_recv)

    @pl.when(core == 0)
    def _():
        wait_for(r.red.at[:, beyond], r.back_recv)

    total = jnp.zeros((per, d.width), F32)
    for p in range(2):
        for k in range(window + 1):
            total = total + r.red[p, k * per : (k + 1) * per, :].astype(F32)
    r.gbk[...] = total[:, :half]
    r.gbv[...] = total[:, half:]

    pair[3].wait_recv()
    r.gv[...] = r.gvt[my_rows, :] + r.gin[1].astype(F32)
    pair[2].wait_recv()
    r.gk[...] = r.gkt[my_rows, :] + r.gin[0].astype(F32)

    for copy in pair:
        copy.wait_send()
    cores[0].wait_send()
    cores[2].wait_send()

    @pl.when(core == 0)
    def _():
        cores[3].wait_send()
        for copy in own_chip:
            copy.wait_send()

    @pl.when(core == 1)
    def _():
        cores[1].wait_send()
        for copy in own_back:
            copy.wait_send()

    wait_for(r.b_in, r.b_send)
    wait_for(r.g_out, r.g_send)


def write_out(*refs):
    sources, results, sems = refs[:5], refs[5:10], refs[10]
    copies = [
        pltpu.make_async_copy(s, o, sems.at[i]) for i, (s, o) in enumerate(zip(sources, results))
    ]
    for copy in copies:
        copy.start()
    for copy in copies:
        copy.wait()


def dims(n_ctx, span, lanes, half, per):
    width = 2 * half
    window = min(8, n_ctx // 2 - 1)
    return types.SimpleNamespace(
        n_ctx=n_ctx,
        span=span,
        lanes=lanes,
        half=half,
        per=per,
        width=width,
        heads=lanes // width,
        window=window,
        nb=window * per,
        scale=width ** (-0.5),
        factor=width ** (-0.5) * LOG2E,
    )


def scratch(d):
    vmem = pltpu.VMEM
    dma = pltpu.SemaphoreType.DMA
    return dict(
        q=vmem((d.span, d.lanes), BF16),
        do=vmem((d.span, d.lanes), BF16),
        bkhalf=vmem((d.per, d.half), BF16),
        bvhalf=vmem((d.per, d.half), BF16),
        turn=vmem((d.span,), jnp.int32),
        chat=pltpu.SMEM((d.n_ctx,), jnp.int32),
        qt=vmem((d.heads, d.width, d.span), BF16),
        dot_t=vmem((d.heads, d.width, d.span), BF16),
        bias=vmem((d.span, d.span), F32),
        kfull=vmem((d.width, d.span), BF16),
        vfull=vmem((d.width, d.span), BF16),
        kt=vmem((d.span, d.width), BF16),
        vt=vmem((d.span, d.width), BF16),
        beacon_out=vmem((d.per, d.width), BF16),
        b_in=vmem((2, d.nb, d.width), BF16),
        b_sib=vmem((2, d.nb, d.width), BF16),
        bkv=vmem((2 * d.nb, 2 * d.width), BF16),
        bkey=vmem((d.width, 2 * d.nb), BF16),
        e_raw=vmem((d.heads, d.span, d.span), F32),
        e_b=vmem((d.heads, 2 * d.nb, d.span), F32),
        dp_raw=vmem((d.heads, d.span, d.span), F32),
        dp_b=vmem((d.heads, 2 * d.nb, d.span), F32),
        p_raw=vmem((d.heads, d.span, d.span), BF16),
        p_b=vmem((d.heads, 2 * d.nb, d.span), BF16),
        s_raw=vmem((d.heads, d.span, d.span), BF16),
        s_b=vmem((d.heads, 2 * d.nb, d.span), BF16),
        stats=vmem((d.heads, 16, d.span), F32),
        gkt=vmem((d.width, d.span), F32),
        gvt=vmem((d.width, d.span), F32),
        gout=vmem((2, d.half, d.span), BF16),
        gin=vmem((2, d.half, d.span), BF16),
        x_out=vmem((d.nb, 2 * d.width), BF16),
        x_in=vmem((d.nb, 2 * d.width), BF16),
        own_out=vmem((2, d.per, d.width), BF16),
        g_out=vmem((2, d.nb, d.width), BF16),
        red=vmem((2, d.nb + d.per, d.width), BF16),
        load_sem=dma((8,)),
        pair_send=dma((4,)),
        pair_recv=dma((4,)),
        core_send=dma((4,)),
        core_recv=dma((4,)),
        own_send=dma((2,)),
        own_recv=dma,
        back_send=dma((2,)),
        back_recv=dma,
        b_send=dma,
        b_recv=dma,
        g_send=dma,
        g_recv=dma,
    )


IN_NAMES = ("chat_hbm", "q_hbm", "do_hbm", "k_hbm", "v_hbm", "bk_hbm", "bv_hbm", "turn_hbm")
OUT_NAMES = ("gq", "gk", "gv", "gbk", "gbv")


def on_device(
    n_ctx, query, grad_out, key_raw, value_raw, beacon_key, beacon_value, chat_of_span, turn_begin
):
    span, lanes = query.shape
    half, per = beacon_key.shape
    d = dims(n_ctx, span, lanes, half, per)
    space = scratch(d)
    hbm = pl.BlockSpec(memory_space=pltpu.HBM)
    vmem = pl.BlockSpec(memory_space=pltpu.VMEM)
    shapes = (
        jax.ShapeDtypeStruct((span, lanes), BF16),
        jax.ShapeDtypeStruct((half, span), F32),
        jax.ShapeDtypeStruct((half, span), F32),
        jax.ShapeDtypeStruct((per, half), F32),
        jax.ShapeDtypeStruct((per, half), F32),
    )
    operands = (
        chat_of_span,
        query,
        grad_out,
        key_raw,
        value_raw,
        beacon_key.T,
        beacon_value.T,
        turn_begin,
    )
    results = pl.pallas_call(
        functools.partial(kernel, IN_NAMES + OUT_NAMES + tuple(space), d),
        out_shape=shapes,
        in_specs=[hbm] * 8,
        out_specs=[vmem] * 5,
        scratch_shapes=list(space.values()),
        compiler_params=pltpu.CompilerParams(
            collective_id=0, has_side_effects=True, vmem_limit_bytes=48 * 1024 * 1024
        ),
        cost_estimate=pl.CostEstimate(
            flops=10 * d.heads * span * (span + 2 * d.nb) * d.width,
            bytes_accessed=6 * span * lanes,
            transcendentals=d.heads * span * (span + 2 * d.nb),
        ),
        name="beacon_backward",
    )(*[pltpu.with_memory_space_constraint(a, pltpu.HBM) for a in operands])
    results = pl.pallas_call(
        write_out,
        out_shape=shapes,
        in_specs=[vmem] * 5,
        out_specs=[hbm] * 5,
        scratch_shapes=[pltpu.SemaphoreType.DMA((5,))],
        name="write_out",
    )(*results)
    return (*results[:3], results[3].T, results[4].T)


def solution(mesh):
    in_specs = (
        P("ctx", "group"),
        P("ctx", "group"),
        P("group", "ctx"),
        P("group", "ctx"),
        P("group", "ctx"),
        P("group", "ctx"),
        P(),
        P("ctx"),
    )
    out_specs = (
        P("ctx", "group"),
        P("group", "ctx"),
        P("group", "ctx"),
        P("group", "ctx"),
        P("group", "ctx"),
    )
    return jax.shard_map(
        functools.partial(on_device, mesh.shape["ctx"]),
        mesh=mesh,
        in_specs=in_specs,
        out_specs=out_specs,
        check_vma=False,
    )
```

```python
import functools
import math
import types

import jax
import jax.numpy as jnp
from jax import lax
from jax.experimental import pallas as pl
from jax.experimental.pallas import tpu as pltpu
from jax.sharding import PartitionSpec as P

MESH = pl.DeviceIdType.MESH
F32 = jnp.float32
BF16 = jnp.bfloat16
HIDDEN = -1e30
BLOCK = 128
LOG2E = math.log2(math.e)


def dot(a, b):
    return lax.dot_general(a, b, (((1,), (0,)), ((), ())), preferred_element_type=F32)


def head_lanes(h, width):
    return slice(h * width, (h + 1) * width)


def turn_queries(r, d):
    for h in range(d.heads):
        r.qt[h] = r.q[:, head_lanes(h, d.width)].T
        r.dot_t[h] = r.do[:, head_lanes(h, d.width)].T


def hide_tokens(r, d):
    begin = r.turn[...].reshape(1, d.span)
    rows = lax.broadcasted_iota(jnp.int32, (BLOCK, d.span), 0)
    cols = lax.broadcasted_iota(jnp.int32, (BLOCK, d.span), 1)
    for lo in range(0, d.span, BLOCK):
        at = rows + lo
        seen = (at <= cols) & (at >= begin)
        r.bias[lo : lo + BLOCK, :] = jnp.where(seen, 0.0, HIDDEN)


def widen(row, lo, fill):
    if lo == 0:
        return row
    return jnp.concatenate([jnp.full((1, lo), fill, F32), row], axis=1)


def raw_part(r, d, h):
    top = jnp.full((1, d.span), HIDDEN, F32)
    for lo in range(0, d.span, BLOCK):
        hi = lo + BLOCK
        s = dot(r.kt[lo:hi, :], r.qt[h, :, lo:]) * d.factor + r.bias[lo:hi, lo:]
        r.e_raw[h, lo:hi, lo:] = s
        top = jnp.maximum(top, widen(jnp.max(s, axis=0, keepdims=True), lo, HIDDEN))
    total = jnp.zeros((1, d.span), F32)
    delta = jnp.zeros((1, d.span), F32)
    for lo in range(0, d.span, BLOCK):
        hi = lo + BLOCK
        e = jnp.exp2(r.e_raw[h, lo:hi, lo:] - top[:, lo:])
        r.e_raw[h, lo:hi, lo:] = e
        g = dot(r.vt[lo:hi, :], r.dot_t[h, :, lo:])
        r.dp_raw[h, lo:hi, lo:] = g
        total = total + widen(jnp.sum(e, axis=0, keepdims=True), lo, 0.0)
        delta = delta + widen(jnp.sum(e * g, axis=0, keepdims=True), lo, 0.0)
    r.stats[h, 0:1, :] = top
    r.stats[h, 1:2, :] = total
    r.stats[h, 2:3, :] = delta


def blocks_of(d, part):
    base = part * d.nb
    return [(lo, min(lo + BLOCK, base + d.nb)) for lo in range(base, base + d.nb, BLOCK)]


def slot_shifts(r, d, me, part):
    core = lax.rem(me, 2)
    chat = r.chat[me]
    shifts = []
    for k in range(1, d.window + 1):
        if part == 0:
            span_id = me - 2 * k
        elif k < d.window:
            span_id = me + 1 - 2 * core - 2 * k
        else:
            span_id = me - core + (1 - core) * (1 - 2 * k)
        shown = (span_id >= 0) & (r.chat[jnp.maximum(span_id, 0)] == chat)
        shifts.append(jnp.where(shown, 0.0, HIDDEN).astype(F32))
    return shifts


def beacon_part(r, d, h, part, shifts):
    top = jnp.full((1, d.span), HIDDEN, F32)
    for lo, hi in blocks_of(d, part):
        s = dot(r.bkv[lo:hi, : d.width], r.qt[h]) * d.factor
        for at in range(lo, hi, d.per):
            moved = s[at - lo : at - lo + d.per] + shifts[(at - part * d.nb) // d.per]
            r.e_b[h, at : at + d.per, :] = moved
            top = jnp.maximum(top, jnp.max(moved, axis=0, keepdims=True))
    total = jnp.zeros((1, d.span), F32)
    delta = jnp.zeros((1, d.span), F32)
    for lo, hi in blocks_of(d, part):
        e = jnp.exp2(r.e_b[h, lo:hi, :] - top)
        r.e_b[h, lo:hi, :] = e
        g = dot(r.bkv[lo:hi, d.width :], r.dot_t[h])
        r.dp_b[h, lo:hi, :] = g
        total = total + jnp.sum(e, axis=0, keepdims=True)
        delta = delta + jnp.sum(e * g, axis=0, keepdims=True)
    at = 3 * (part + 1)
    r.stats[h, at : at + 1, :] = top
    r.stats[h, at + 1 : at + 2, :] = total
    r.stats[h, at + 2 : at + 3, :] = delta


def combine(r, d, h):
    tops = [r.stats[h, i : i + 1, :] for i in (0, 3, 6)]
    top = jnp.maximum(jnp.maximum(tops[0], tops[1]), tops[2])
    factors = [jnp.exp2(t - top) for t in tops]
    total = jnp.zeros((1, d.span), F32)
    delta = jnp.zeros((1, d.span), F32)
    for i, f in enumerate(factors):
        total = total + f * r.stats[h, 3 * i + 1 : 3 * i + 2, :]
        delta = delta + f * r.stats[h, 3 * i + 2 : 3 * i + 3, :]
    inv = 1.0 / total
    for i, f in enumerate(factors):
        r.stats[h, 9 + i : 10 + i, :] = f * inv
    r.stats[h, 12:13, :] = delta * inv


def beacon_grads(r, d, part):
    for lo, hi in blocks_of(d, part):
        gk = jnp.zeros((hi - lo, d.width), F32)
        gv = jnp.zeros((hi - lo, d.width), F32)
        for h in range(d.heads):
            p = r.e_b[h, lo:hi, :] * r.stats[h, 10 + part : 11 + part, :]
            s = (p * (r.dp_b[h, lo:hi, :] - r.stats[h, 12:13, :])).astype(BF16)
            r.s_b[h, lo:hi, :] = s
            gk = gk + dot(s, r.q[:, head_lanes(h, d.width)])
            gv = gv + dot(p.astype(BF16), r.do[:, head_lanes(h, d.width)])
        yield lo - part * d.nb, hi - part * d.nb, gk * d.scale, gv


def pack_halves(ref, at, gk, gv, half):
    ref[0, at, :] = jnp.concatenate([gk[:, :half], gv[:, :half]], axis=1).astype(BF16)
    ref[1, at, :] = jnp.concatenate([gk[:, half:], gv[:, half:]], axis=1).astype(BF16)


def raw_grads(r, d, lo):
    hi = lo + BLOCK
    gk = jnp.zeros((BLOCK, d.width), F32)
    gv = jnp.zeros((BLOCK, d.width), F32)
    for h in range(d.heads):
        p = r.e_raw[h, lo:hi, lo:] * r.stats[h, 9:10, lo:]
        s = (p * (r.dp_raw[h, lo:hi, lo:] - r.stats[h, 12:13, lo:])).astype(BF16)
        r.s_raw[h, lo:hi, lo:] = s
        if lo % (2 * BLOCK):
            r.s_raw[h, lo:hi, lo - BLOCK : lo] = jnp.zeros((BLOCK, BLOCK), BF16)
        gk = gk + dot(s, r.q[lo:, head_lanes(h, d.width)])
        gv = gv + dot(p.astype(BF16), r.do[lo:, head_lanes(h, d.width)])
    r.gkt[:, lo:hi] = (gk * d.scale).T
    r.gvt[:, lo:hi] = gv.T


def query_grads(r, d, h):
    for lo in range(0, d.span, 2 * BLOCK):
        hi = lo + 2 * BLOCK
        g = dot(r.kfull[:, :hi], r.s_raw[h, :hi, lo:hi]) + dot(r.bkey[...], r.s_b[h, :, lo:hi])
        r.gq[lo:hi, head_lanes(h, d.width)] = (g * d.scale).T.astype(BF16)


def unfold(r, d, part, halves):
    low, high = halves[0], halves[1]
    half = d.half
    r.bkv[part * d.nb : (part + 1) * d.nb, :] = jnp.concatenate(
        [low[:, :half], high[:, :half], low[:, half:], high[:, half:]], axis=1
    )


def wait_for(ref, sem):
    pltpu.make_async_copy(ref, ref, sem).wait()


def kernel(names, d, *refs):
    r = types.SimpleNamespace(**dict(zip(names, refs)))
    per, half, window, n_ctx = d.per, d.half, d.window, d.n_ctx

    z = lax.axis_index("group")
    me = lax.axis_index("ctx")
    parity = lax.rem(z, 2)
    even = z - parity
    partner = z + 1 - 2 * parity
    core = lax.rem(me, 2)
    sibling = me + 1 - 2 * core
    my_rows = pl.ds(parity * half, half)
    their_rows = pl.ds((1 - parity) * half, half)
    shared = pl.ds(0, (window - 1) * per)
    last = pl.ds((window - 1) * per, per)
    beyond = pl.ds(window * per, per)

    barrier = pltpu.get_barrier_semaphore()

    def greet(group, ctx):
        pl.semaphore_signal(barrier, inc=1, device_id=(group, ctx), device_id_type=MESH)

    def greet_earlier(i, carry):
        k = window - i // 2
        greet(even + lax.rem(i, 2), lax.rem(me + n_ctx - 2 * k, n_ctx))
        return carry

    lax.fori_loop(0, 2 * window, greet_earlier, 0)
    greet(partner, me)
    greet(z, sibling)
    greet(partner, sibling)

    loads = [
        pltpu.make_async_copy(src, dst, r.load_sem.at[i])
        for i, (src, dst) in enumerate(
            (
                (r.bk_hbm, r.bkhalf),
                (r.bv_hbm, r.bvhalf),
                (r.k_hbm, r.kfull.at[my_rows]),
                (r.v_hbm, r.vfull.at[my_rows]),
                (r.q_hbm, r.q),
                (r.do_hbm, r.do),
                (r.turn_hbm, r.turn),
                (r.chat_hbm, r.chat),
            )
        )
    ]
    for copy in loads:
        copy.start()

    loads[0].wait()
    loads[1].wait()
    r.beacon_out[...] = jnp.concatenate([r.bkhalf[...], r.bvhalf[...]], axis=1)
    loads[2].wait()
    loads[3].wait()
    pl.semaphore_wait(barrier, 2 * window + 3)

    def remote(src, dst, send, recv, group, ctx):
        return pltpu.make_async_remote_copy(
            src_ref=src,
            dst_ref=dst,
            send_sem=send,
            recv_sem=recv,
            device_id=(group, ctx),
            device_id_type=MESH,
        )

    def to_partner(i, src, dst):
        return remote(src, dst, r.pair_send.at[i], r.pair_recv.at[i], partner, me)

    def to_sibling(i, src, dst):
        return remote(src, dst, r.core_send.at[i], r.core_recv.at[i], z, sibling)

    pair = [
        to_partner(0, r.kfull.at[my_rows], r.kfull.at[my_rows]),
        to_partner(1, r.vfull.at[my_rows], r.vfull.at[my_rows]),
    ]
    raw_blocks = range(0, d.span, BLOCK)
    pair_back = [
        to_partner(
            2 + i, r.gout.at[:, :, pl.ds(lo, BLOCK)], r.gin.at[:, :, pl.ds(lo, BLOCK)]
        )
        for i, lo in enumerate(raw_blocks)
    ]
    cores = [
        to_sibling(0, r.b_in.at[:, shared], r.b_sib.at[:, shared]),
        to_sibling(1, r.b_in.at[:, last], r.b_sib.at[:, last]),
        to_sibling(2, r.x_out.at[shared], r.x_in.at[shared]),
        to_sibling(3, r.x_out.at[last], r.x_in.at[last]),
    ]

    pair[0].start()

    def push(i, carry):
        k = window - i // 2
        remote(
            r.beacon_out,
            r.b_in.at[parity, pl.ds((k - 1) * per, per)],
            r.b_send,
            r.b_recv,
            even + lax.rem(i, 2),
            lax.rem(me + 2 * k, n_ctx),
        ).start()
        return carry

    lax.fori_loop(0, 2 * window, push, 0)
    pair[1].start()

    own_chip = [
        remote(
            r.beacon_out,
            r.b_sib.at[parity, last],
            r.own_send.at[i],
            r.own_recv,
            group,
            sibling,
        )
        for i, group in enumerate((z, partner))
    ]

    @pl.when(core == 0)
    def _():
        for copy in own_chip:
            copy.start()

    for i in (4, 5, 6, 7):
        loads[i].wait()
    turn_queries(r, d)
    hide_tokens(r, d)

    @pl.when(core == 0)
    def _():
        r.x_in[last, :] = jnp.zeros((per, 2 * d.width), BF16)

    @pl.when(core == 1)
    def _():
        r.red[:, beyond, :] = jnp.zeros((2, per, d.width), BF16)

    pair[0].wait_recv()
    r.kt[...] = r.kfull[...].T
    pair[1].wait_recv()
    r.vt[...] = r.vfull[...].T
    for h in range(d.heads):
        raw_part(r, d, h)

    wait_for(r.b_in, r.b_recv)
    cores[0].start()

    @pl.when(core == 1)
    def _():
        cores[1].start()

    unfold(r, d, 0, r.b_in)
    shifts = slot_shifts(r, d, me, 0)
    for h in range(d.heads):
        beacon_part(r, d, h, 0, shifts)

    cores[0].wait_recv()

    @pl.when(core == 0)
    def _():
        cores[1].wait_recv()

    @pl.when(core == 1)
    def _():
        wait_for(r.b_sib.at[:, last], r.own_recv)

    unfold(r, d, 1, r.b_sib)
    shifts_sib = slot_shifts(r, d, me, 1)

    for h in range(d.heads):
        beacon_part(r, d, h, 1, shifts_sib)
        combine(r, d, h)

    for lo, hi, gk, gv in beacon_grads(r, d, 1):
        r.x_out[lo:hi, : d.width] = gk.astype(BF16)
        r.x_out[lo:hi, d.width :] = gv.astype(BF16)
    cores[2].start()

    @pl.when(core == 0)
    def _():
        cores[3].start()

    tail = r.x_out[last, :]
    pack_halves(r.own_out, slice(None), tail[:, : d.width], tail[:, d.width :], half)
    own_back = [
        remote(
            r.own_out.at[p],
            r.red.at[parity, beyond],
            r.back_send.at[p],
            r.back_recv,
            even + p,
            sibling,
        )
        for p in range(2)
    ]

    @pl.when(core == 1)
    def _():
        for copy in own_back:
            copy.start()

    for lo, hi, gk, gv in beacon_grads(r, d, 0):
        r.g_own[lo:hi, : d.width] = gk
        r.g_own[lo:hi, d.width :] = gv
    cores[2].wait_recv()

    @pl.when(core == 1)
    def _():
        cores[3].wait_recv()

    total = r.g_own[...] + r.x_in[...].astype(F32)
    pack_halves(r.g_out, slice(None), total[:, : d.width], total[:, d.width :], half)

    def push_back(i, carry):
        k = window - i // 2
        p = lax.rem(i, 2)
        at = pl.ds((k - 1) * per, per)
        remote(
            r.g_out.at[p, at],
            r.red.at[parity, at],
            r.g_send,
            r.g_recv,
            even + p,
            lax.rem(me + n_ctx - 2 * k, n_ctx),
        ).start()
        return carry

    lax.fori_loop(0, 2 * window, push_back, 0)

    for copy, lo in zip(pair_back, raw_blocks):
        raw_grads(r, d, lo)
        r.gout[0, :, lo : lo + BLOCK] = r.gkt[their_rows, lo : lo + BLOCK].astype(BF16)
        r.gout[1, :, lo : lo + BLOCK] = r.gvt[their_rows, lo : lo + BLOCK].astype(BF16)
        copy.start()

    r.bkey[...] = r.bkv[:, : d.width].T
    for h in range(d.heads):
        query_grads(r, d, h)

    whole = pl.ds(0, window * per)
    wait_for(r.red.at[:, whole], r.g_recv)

    @pl.when(core == 0)
    def _():
        wait_for(r.red.at[:, beyond], r.back_recv)

    total = jnp.zeros((per, d.width), F32)
    for p in range(2):
        for k in range(window + 1):
            total = total + r.red[p, k * per : (k + 1) * per, :].astype(F32)
    r.gbk[...] = total[:, :half]
    r.gbv[...] = total[:, half:]

    for copy in pair_back:
        copy.wait_recv()
    r.gk[...] = r.gkt[my_rows, :] + r.gin[0].astype(F32)
    r.gv[...] = r.gvt[my_rows, :] + r.gin[1].astype(F32)

    for copy in pair + pair_back:
        copy.wait_send()
    cores[0].wait_send()
    cores[2].wait_send()

    @pl.when(core == 0)
    def _():
        cores[3].wait_send()
        for copy in own_chip:
            copy.wait_send()

    @pl.when(core == 1)
    def _():
        cores[1].wait_send()
        for copy in own_back:
            copy.wait_send()

    wait_for(r.b_in, r.b_send)
    wait_for(r.g_out, r.g_send)


def write_out(*refs):
    sources, results, sems = refs[:5], refs[5:10], refs[10]
    copies = [
        pltpu.make_async_copy(s, o, sems.at[i]) for i, (s, o) in enumerate(zip(sources, results))
    ]
    for copy in copies:
        copy.start()
    for copy in copies:
        copy.wait()


def dims(n_ctx, span, lanes, half, per):
    width = 2 * half
    window = min(8, n_ctx // 2 - 1)
    return types.SimpleNamespace(
        n_ctx=n_ctx,
        span=span,
        lanes=lanes,
        half=half,
        per=per,
        width=width,
        heads=lanes // width,
        window=window,
        nb=window * per,
        scale=width ** (-0.5),
        factor=width ** (-0.5) * LOG2E,
    )


def scratch(d):
    vmem = pltpu.VMEM
    dma = pltpu.SemaphoreType.DMA
    return dict(
        q=vmem((d.span, d.lanes), BF16),
        do=vmem((d.span, d.lanes), BF16),
        bkhalf=vmem((d.per, d.half), BF16),
        bvhalf=vmem((d.per, d.half), BF16),
        turn=vmem((d.span,), jnp.int32),
        chat=pltpu.SMEM((d.n_ctx,), jnp.int32),
        qt=vmem((d.heads, d.width, d.span), BF16),
        dot_t=vmem((d.heads, d.width, d.span), BF16),
        bias=vmem((d.span, d.span), F32),
        kfull=vmem((d.width, d.span), BF16),
        vfull=vmem((d.width, d.span), BF16),
        kt=vmem((d.span, d.width), BF16),
        vt=vmem((d.span, d.width), BF16),
        beacon_out=vmem((d.per, d.width), BF16),
        b_in=vmem((2, d.nb, d.width), BF16),
        b_sib=vmem((2, d.nb, d.width), BF16),
        bkv=vmem((2 * d.nb, 2 * d.width), BF16),
        bkey=vmem((d.width, 2 * d.nb), BF16),
        e_raw=vmem((d.heads, d.span, d.span), F32),
        e_b=vmem((d.heads, 2 * d.nb, d.span), F32),
        dp_raw=vmem((d.heads, d.span, d.span), F32),
        dp_b=vmem((d.heads, 2 * d.nb, d.span), F32),
        s_raw=vmem((d.heads, d.span, d.span), BF16),
        s_b=vmem((d.heads, 2 * d.nb, d.span), BF16),
        stats=vmem((d.heads, 16, d.span), F32),
        gkt=vmem((d.width, d.span), F32),
        gvt=vmem((d.width, d.span), F32),
        gout=vmem((2, d.half, d.span), BF16),
        gin=vmem((2, d.half, d.span), BF16),
        x_out=vmem((d.nb, 2 * d.width), BF16),
        x_in=vmem((d.nb, 2 * d.width), BF16),
        own_out=vmem((2, d.per, d.width), BF16),
        g_own=vmem((d.nb, 2 * d.width), F32),
        g_out=vmem((2, d.nb, d.width), BF16),
        red=vmem((2, d.nb + d.per, d.width), BF16),
        load_sem=dma((8,)),
        pair_send=dma((6,)),
        pair_recv=dma((6,)),
        core_send=dma((4,)),
        core_recv=dma((4,)),
        own_send=dma((2,)),
        own_recv=dma,
        back_send=dma((2,)),
        back_recv=dma,
        b_send=dma,
        b_recv=dma,
        g_send=dma,
        g_recv=dma,
    )


IN_NAMES = ("chat_hbm", "q_hbm", "do_hbm", "k_hbm", "v_hbm", "bk_hbm", "bv_hbm", "turn_hbm")
OUT_NAMES = ("gq", "gk", "gv", "gbk", "gbv")


def on_device(
    n_ctx, query, grad_out, key_raw, value_raw, beacon_key, beacon_value, chat_of_span, turn_begin
):
    span, lanes = query.shape
    half, per = beacon_key.shape
    d = dims(n_ctx, span, lanes, half, per)
    space = scratch(d)
    hbm = pl.BlockSpec(memory_space=pltpu.HBM)
    vmem = pl.BlockSpec(memory_space=pltpu.VMEM)
    shapes = (
        jax.ShapeDtypeStruct((span, lanes), BF16),
        jax.ShapeDtypeStruct((half, span), F32),
        jax.ShapeDtypeStruct((half, span), F32),
        jax.ShapeDtypeStruct((per, half), F32),
        jax.ShapeDtypeStruct((per, half), F32),
    )
    operands = (
        chat_of_span,
        query,
        grad_out,
        key_raw,
        value_raw,
        beacon_key.T,
        beacon_value.T,
        turn_begin,
    )
    results = pl.pallas_call(
        functools.partial(kernel, IN_NAMES + OUT_NAMES + tuple(space), d),
        out_shape=shapes,
        in_specs=[hbm] * 8,
        out_specs=[vmem] * 5,
        scratch_shapes=list(space.values()),
        compiler_params=pltpu.CompilerParams(
            collective_id=0, has_side_effects=True, vmem_limit_bytes=48 * 1024 * 1024
        ),
        cost_estimate=pl.CostEstimate(
            flops=10 * d.heads * span * (span + 2 * d.nb) * d.width,
            bytes_accessed=6 * span * lanes,
            transcendentals=d.heads * span * (span + 2 * d.nb),
        ),
        name="beacon_backward",
    )(*[pltpu.with_memory_space_constraint(a, pltpu.HBM) for a in operands])
    results = pl.pallas_call(
        write_out,
        out_shape=shapes,
        in_specs=[vmem] * 5,
        out_specs=[hbm] * 5,
        scratch_shapes=[pltpu.SemaphoreType.DMA((5,))],
        compiler_params=pltpu.CompilerParams(vmem_limit_bytes=2 * 1024 * 1024),
        name="write_out",
    )(*results)
    return (*results[:3], results[3].T, results[4].T)


def solution(mesh):
    in_specs = (
        P("ctx", "group"),
        P("ctx", "group"),
        P("group", "ctx"),
        P("group", "ctx"),
        P("group", "ctx"),
        P("group", "ctx"),
        P(),
        P("ctx"),
    )
    out_specs = (
        P("ctx", "group"),
        P("group", "ctx"),
        P("group", "ctx"),
        P("group", "ctx"),
        P("group", "ctx"),
    )
    return jax.shard_map(
        functools.partial(on_device, mesh.shape["ctx"]),
        mesh=mesh,
        in_specs=in_specs,
        out_specs=out_specs,
        check_vma=False,
    )
```

```python
import functools
import math
import types

import jax
import jax.numpy as jnp
from jax import lax
from jax.experimental import pallas as pl
from jax.experimental.pallas import tpu as pltpu
from jax.sharding import PartitionSpec as P

MESH = pl.DeviceIdType.MESH
F32 = jnp.float32
BF16 = jnp.bfloat16
HIDDEN = -1e30
BLOCK = 128
LOG2E = math.log2(math.e)


def dot(a, b):
    return lax.dot_general(a, b, (((1,), (0,)), ((), ())), preferred_element_type=F32)


def head_lanes(h, width):
    return slice(h * width, (h + 1) * width)


def turn_queries(r, d):
    for h in range(d.heads):
        r.qt[h] = r.q[:, head_lanes(h, d.width)].T
        r.dot_t[h] = r.do[:, head_lanes(h, d.width)].T


def hide_tokens(r, d):
    begin = r.turn[...].reshape(1, d.span)
    rows = lax.broadcasted_iota(jnp.int32, (BLOCK, d.span), 0)
    cols = lax.broadcasted_iota(jnp.int32, (BLOCK, d.span), 1)
    for lo in range(0, d.span, BLOCK):
        at = rows + lo
        seen = (at <= cols) & (at >= begin)
        r.bias[lo : lo + BLOCK, :] = jnp.where(seen, 0.0, HIDDEN)


def note(r, h, part, lo, top, e, g):
    rows = (top, jnp.sum(e, axis=0, keepdims=True), jnp.sum(e * g, axis=0, keepdims=True))
    for i, row in enumerate(rows):
        r.stats[h, 3 * part + i : 3 * part + i + 1, lo:] = row
        if lo:
            fill = jnp.full((1, lo), HIDDEN if i == 0 else 0.0, F32)
            r.stats[h, 3 * part + i : 3 * part + i + 1, :lo] = fill


def raw_part(r, d, h, part):
    lo, hi = part * BLOCK, (part + 1) * BLOCK
    s = dot(r.kt[lo:hi, :], r.qt[h, :, lo:]) * d.factor + r.bias[lo:hi, lo:]
    r.e_raw[h, lo:hi, lo:] = s
    top = jnp.max(s, axis=0, keepdims=True)
    e = jnp.exp2(r.e_raw[h, lo:hi, lo:] - top)
    r.e_raw[h, lo:hi, lo:] = e
    g = dot(r.vt[lo:hi, :], r.dot_t[h, :, lo:])
    r.dp_raw[h, lo:hi, lo:] = g
    note(r, h, part, lo, top, e, g)


def slot_shift(r, d, me, side, slot):
    core = lax.rem(me, 2)
    k = d.order[slot]
    if side == 0:
        span_id = me - 2 * k
    elif k < d.window:
        span_id = me + 1 - 2 * core - 2 * k
    else:
        span_id = me - core + (1 - core) * (1 - 2 * k)
    shown = (span_id >= 0) & (r.chat[jnp.maximum(span_id, 0)] == r.chat[me])
    return jnp.where(shown, 0.0, HIDDEN).astype(F32)


def part_of(d, side, group):
    first, end = d.groups[group]
    base = side * d.nb
    return d.raws + 2 * side + group, first, base + first * d.per, base + end * d.per


def beacon_part(r, d, h, side, group, shifts):
    part, _, lo, hi = part_of(d, side, group)
    top = jnp.full((1, d.span), HIDDEN, F32)
    s = dot(r.bkv[lo:hi, : d.width], r.qt[h]) * d.factor
    for i, shift in enumerate(shifts):
        moved = s[i * d.per : (i + 1) * d.per] + shift
        r.e_b[h, lo + i * d.per : lo + (i + 1) * d.per, :] = moved
        top = jnp.maximum(top, jnp.max(moved, axis=0, keepdims=True))
    e = jnp.exp2(r.e_b[h, lo:hi, :] - top)
    r.e_b[h, lo:hi, :] = e
    g = dot(r.bkv[lo:hi, d.width :], r.dot_t[h])
    r.dp_b[h, lo:hi, :] = g
    note(r, h, part, 0, top, e, g)


def combine(r, d, h):
    tops = [r.stats[h, 3 * i : 3 * i + 1, :] for i in range(d.parts)]
    top = functools.reduce(jnp.maximum, tops)
    factors = [jnp.exp2(t - top) for t in tops]
    total = jnp.zeros((1, d.span), F32)
    delta = jnp.zeros((1, d.span), F32)
    for i, f in enumerate(factors):
        total = total + f * r.stats[h, 3 * i + 1 : 3 * i + 2, :]
        delta = delta + f * r.stats[h, 3 * i + 2 : 3 * i + 3, :]
    inv = 1.0 / total
    for i, f in enumerate(factors):
        r.stats[h, d.factors + i : d.factors + i + 1, :] = f * inv
    r.stats[h, d.delta : d.delta + 1, :] = delta * inv


def beacon_grads(r, d, side, group):
    part, _, lo, hi = part_of(d, side, group)
    gk = jnp.zeros((hi - lo, d.width), F32)
    gv = jnp.zeros((hi - lo, d.width), F32)
    for h in range(d.heads):
        p = r.e_b[h, lo:hi, :] * r.stats[h, d.factors + part : d.factors + part + 1, :]
        s = (p * (r.dp_b[h, lo:hi, :] - r.stats[h, d.delta : d.delta + 1, :])).astype(BF16)
        r.s_b[h, lo:hi, :] = s
        gk = gk + dot(s, r.q[:, head_lanes(h, d.width)])
        gv = gv + dot(p.astype(BF16), r.do[:, head_lanes(h, d.width)])
    return gk * d.scale, gv


def pack_halves(ref, at, gk, gv, half):
    ref[0, at, :] = jnp.concatenate([gk[:, :half], gv[:, :half]], axis=1).astype(BF16)
    ref[1, at, :] = jnp.concatenate([gk[:, half:], gv[:, half:]], axis=1).astype(BF16)


def raw_grads(r, d, lo):
    hi = lo + BLOCK
    at = d.factors + lo // BLOCK
    gk = jnp.zeros((BLOCK, d.width), F32)
    gv = jnp.zeros((BLOCK, d.width), F32)
    for h in range(d.heads):
        p = r.e_raw[h, lo:hi, lo:] * r.stats[h, at : at + 1, lo:]
        s = (p * (r.dp_raw[h, lo:hi, lo:] - r.stats[h, d.delta : d.delta + 1, lo:])).astype(BF16)
        r.s_raw[h, lo:hi, lo:] = s
        if lo % (2 * BLOCK):
            r.s_raw[h, lo:hi, lo - BLOCK : lo] = jnp.zeros((BLOCK, BLOCK), BF16)
        gk = gk + dot(s, r.q[lo:, head_lanes(h, d.width)])
        gv = gv + dot(p.astype(BF16), r.do[lo:, head_lanes(h, d.width)])
    r.gkt[:, lo:hi] = (gk * d.scale).T
    r.gvt[:, lo:hi] = gv.T


def query_grads(r, d, h):
    for lo in range(0, d.span, 2 * BLOCK):
        hi = lo + 2 * BLOCK
        g = dot(r.kv[0, :, :hi], r.s_raw[h, :hi, lo:hi]) + dot(r.bkey[...], r.s_b[h, :, lo:hi])
        r.gq[lo:hi, head_lanes(h, d.width)] = (g * d.scale).T.astype(BF16)


def unfold(r, d, side, group, halves):
    _, _, lo, hi = part_of(d, side, group)
    at = slice(lo - side * d.nb, hi - side * d.nb)
    low, high = halves[0, at, :], halves[1, at, :]
    half = d.half
    r.bkv[lo:hi, :] = jnp.concatenate(
        [low[:, :half], high[:, :half], low[:, half:], high[:, half:]], axis=1
    )


def wait_for(ref, sem):
    pltpu.make_async_copy(ref, ref, sem).wait()


def kernel(names, d, *refs):
    r = types.SimpleNamespace(**dict(zip(names, refs)))
    per, half, window, n_ctx = d.per, d.half, d.window, d.n_ctx

    z = lax.axis_index("group")
    me = lax.axis_index("ctx")
    parity = lax.rem(z, 2)
    even = z - parity
    partner = z + 1 - 2 * parity
    core = lax.rem(me, 2)
    sibling = me + 1 - 2 * core
    chip = lax.div(me, 2)
    chips = n_ctx // 2
    my_rows = pl.ds(parity * half, half)
    their_rows = pl.ds((1 - parity) * half, half)
    near = pl.ds(0, d.groups[0][1] * per)
    far = pl.ds(d.groups[0][1] * per, (window - d.groups[0][1]) * per)
    first = pl.ds(0, per)
    shared = pl.ds(per, (d.groups[0][1] - 1) * per)
    beyond = pl.ds(window * per, per)

    barrier = pltpu.get_barrier_semaphore()

    def greet(group, ctx):
        pl.semaphore_signal(barrier, inc=1, device_id=(group, ctx), device_id_type=MESH)

    for k in reversed(d.order):

        @pl.when(chip >= k)
        def _():
            for p in range(2):
                greet(even + p, me - 2 * k)

    greet(partner, me)
    greet(z, sibling)
    greet(partner, sibling)

    loads = [
        pltpu.make_async_copy(src, dst, r.load_sem.at[i])
        for i, (src, dst) in enumerate(
            (
                (r.bk_hbm, r.bkhalf),
                (r.bv_hbm, r.bvhalf),
                (r.k_hbm, r.kv.at[0, my_rows]),
                (r.v_hbm, r.kv.at[1, my_rows]),
                (r.q_hbm, r.q),
                (r.do_hbm, r.do),
                (r.turn_hbm, r.turn),
                (r.chat_hbm, r.chat),
            )
        )
    ]
    for copy in loads:
        copy.start()

    loads[0].wait()
    loads[1].wait()
    r.beacon_out[...] = jnp.concatenate([r.bkhalf[...], r.bvhalf[...]], axis=1)
    loads[2].wait()
    loads[3].wait()
    pl.semaphore_wait(barrier, 2 * jnp.minimum(window, chips - 1 - chip) + 3)

    def remote(src, dst, send, recv, group, ctx):
        return pltpu.make_async_remote_copy(
            src_ref=src,
            dst_ref=dst,
            send_sem=send,
            recv_sem=recv,
            device_id=(group, ctx),
            device_id_type=MESH,
        )

    def to_partner(i, src, dst):
        return remote(src, dst, r.pair_send.at[i], r.pair_recv.at[i], partner, me)

    def to_sibling(i, src, dst):
        return remote(src, dst, r.core_send.at[i], r.core_recv.at[i], z, sibling)

    raw_blocks = range(0, d.span, BLOCK)
    pair = []
    pair_back = []
    mine = r.kv.at[:, my_rows]
    pair.append(to_partner(2 * d.raws, mine, mine))
    for i, lo in enumerate(raw_blocks):
        at = pl.ds(lo, BLOCK)
        pair_back.append(to_partner(d.raws + i, r.gout.at[:, :, at], r.gin.at[:, :, at]))
    cores = [
        to_sibling(0, r.b_in.at[:, shared], r.b_sib.at[:, shared]),
        to_sibling(1, r.b_in.at[:, first], r.b_sib.at[:, first]),
        to_sibling(2, r.b_in.at[:, far], r.b_sib.at[:, far]),
        to_sibling(3, r.x_out.at[far], r.x_in.at[far]),
        to_sibling(4, r.x_out.at[shared], r.x_in.at[shared]),
        to_sibling(5, r.x_out.at[first], r.x_in.at[first]),
    ]


    def push(group):
        for slot in reversed(range(*d.groups[group])):
            k = d.order[slot]

            @pl.when(chip + k < chips)
            def _():
                for p in range(2):
                    remote(
                        r.beacon_out,
                        r.b_in.at[parity, pl.ds(slot * per, per)],
                        r.b_send.at[slot],
                        r.b_recv.at[slot],
                        even + p,
                        me + 2 * k,
                    ).start()

    push(1)
    push(0)
    pair[0].start()

    own_chip = [
        remote(
            r.beacon_out,
            r.b_sib.at[parity, first],
            r.own_send.at[i],
            r.own_recv,
            group,
            sibling,
        )
        for i, group in enumerate((z, partner))
    ]

    @pl.when(core == 0)
    def _():
        for copy in own_chip:
            copy.start()

    for i in (4, 5, 6, 7):
        loads[i].wait()
    turn_queries(r, d)
    hide_tokens(r, d)

    @pl.when(core == 0)
    def _():
        r.x_in[first, :] = jnp.zeros((per, 2 * d.width), BF16)

    @pl.when(core == 1)
    def _():
        r.red[:, beyond, :] = jnp.zeros((2, per, d.width), BF16)

    nothing = jnp.zeros((2, per, d.width), BF16)
    for slot in range(window):
        k = d.order[slot]
        at = pl.ds(slot * per, per)

        @pl.when(chip < k)
        def _():
            r.b_in[:, at, :] = nothing

        @pl.when(chip + k >= chips)
        def _():
            r.red[:, at, :] = nothing


    def shifts(side, group):
        return [slot_shift(r, d, me, side, slot) for slot in range(*d.groups[group])]

    def attend(side, group, halves):
        unfold(r, d, side, group, halves)
        moves = shifts(side, group)
        for h in range(d.heads):
            beacon_part(r, d, h, side, group, moves)

    def raw(part):
        if part == 0:
            pair[0].wait_recv()
        lo, hi = part * BLOCK, (part + 1) * BLOCK
        r.kt[lo:hi, :] = r.kv[0, :, lo:hi].T
        r.vt[lo:hi, :] = r.kv[1, :, lo:hi].T
        for h in range(d.heads):
            raw_part(r, d, h, part)

    def slot_rows(slot):
        return pl.ds(slot * per, per)

    def arrived(group):
        for slot in range(*d.groups[group]):

            @pl.when(chip >= d.order[slot])
            def _():
                wait_for(r.b_in.at[:, slot_rows(slot)], r.b_recv.at[slot])

    def exchange_near():
        arrived(0)
        cores[0].start()

        @pl.when(core == 1)
        def _():
            cores[1].start()

    def exchange_far():
        arrived(1)
        cores[2].start()

    def near_from_sibling():
        cores[0].wait_recv()

        @pl.when(core == 0)
        def _():
            cores[1].wait_recv()

        @pl.when(core == 1)
        def _():
            wait_for(r.b_sib.at[:, first], r.own_recv)

        attend(1, 0, r.b_sib)

    exchange_near()
    exchange_far()
    attend(0, 0, r.b_in)
    attend(0, 1, r.b_in)
    raw(0)
    raw(1)
    near_from_sibling()
    cores[2].wait_recv()
    attend(1, 1, r.b_sib)
    raw(2)
    raw(3)
    for h in range(d.heads):
        combine(r, d, h)

    def to_other_core(group):
        _, _, lo, hi = part_of(d, 0, group)
        gk, gv = beacon_grads(r, d, 1, group)
        r.x_out[lo:hi, : d.width] = gk.astype(BF16)
        r.x_out[lo:hi, d.width :] = gv.astype(BF16)

    own_back = [
        remote(
            r.own_out.at[p],
            r.red.at[parity, beyond],
            r.back_send.at[p],
            r.back_recv,
            even + p,
            sibling,
        )
        for p in range(2)
    ]


    def to_owners(group):
        _, _, lo, hi = part_of(d, 0, group)
        gk = r.g_own[lo:hi, : d.width] + r.x_in[lo:hi, : d.width].astype(F32)
        gv = r.g_own[lo:hi, d.width :] + r.x_in[lo:hi, d.width :].astype(F32)
        pack_halves(r.g_out, slice(lo, hi), gk, gv, half)
        for slot in reversed(range(*d.groups[group])):
            k = d.order[slot]

            @pl.when(chip >= k)
            def _():
                at = pl.ds(slot * per, per)
                for p in range(2):
                    remote(
                        r.g_out.at[p, at],
                        r.red.at[parity, at],
                        r.g_send.at[slot],
                        r.g_recv.at[slot],
                        even + p,
                        me - 2 * k,
                    ).start()

    def raw_back(part):
        lo = part * BLOCK
        raw_grads(r, d, lo)
        r.gout[0, :, lo : lo + BLOCK] = r.gkt[their_rows, lo : lo + BLOCK].astype(BF16)
        r.gout[1, :, lo : lo + BLOCK] = r.gvt[their_rows, lo : lo + BLOCK].astype(BF16)
        pair_back[part].start()

    def far_to_sibling():
        to_other_core(1)
        cores[3].start()

    def near_to_sibling():
        to_other_core(0)
        cores[4].start()

        @pl.when(core == 0)
        def _():
            cores[5].start()

        own = r.x_out[first, :]
        pack_halves(r.own_out, slice(None), own[:, : d.width], own[:, d.width :], half)

        @pl.when(core == 1)
        def _():
            for copy in own_back:
                copy.start()

    def own_grads(group):
        _, _, lo, hi = part_of(d, 0, group)
        gk, gv = beacon_grads(r, d, 0, group)
        r.g_own[lo:hi, : d.width] = gk
        r.g_own[lo:hi, d.width :] = gv

    def far_to_owners():
        cores[3].wait_recv()
        to_owners(1)

    def near_to_owners():
        cores[4].wait_recv()

        @pl.when(core == 1)
        def _():
            cores[5].wait_recv()

        to_owners(0)

    far_to_sibling()
    near_to_sibling()
    own_grads(1)
    far_to_owners()
    raw_back(0)
    own_grads(0)
    near_to_owners()
    raw_back(1)
    raw_back(2)
    raw_back(3)

    r.bkey[...] = r.bkv[:, : d.width].T
    for h in range(d.heads):
        query_grads(r, d, h)

    for slot in range(window):

        @pl.when(chip + d.order[slot] < chips)
        def _():
            wait_for(r.red.at[:, slot_rows(slot)], r.g_recv.at[slot])


    @pl.when(core == 0)
    def _():
        wait_for(r.red.at[:, beyond], r.back_recv)

    total = jnp.zeros((per, d.width), F32)
    for p in range(2):
        for k in range(window + 1):
            total = total + r.red[p, k * per : (k + 1) * per, :].astype(F32)
    r.gbk[...] = total[:, :half]
    r.gbv[...] = total[:, half:]

    for copy in pair_back:
        copy.wait_recv()
    r.gk[...] = r.gkt[my_rows, :] + r.gin[0].astype(F32)
    r.gv[...] = r.gvt[my_rows, :] + r.gin[1].astype(F32)

    for copy in pair + pair_back:
        copy.wait_send()
    for i in (0, 2, 3, 4):
        cores[i].wait_send()

    @pl.when(core == 0)
    def _():
        cores[5].wait_send()
        for copy in own_chip:
            copy.wait_send()

    @pl.when(core == 1)
    def _():
        cores[1].wait_send()
        for copy in own_back:
            copy.wait_send()

    for slot in range(window):
        k = d.order[slot]

        @pl.when(chip + k < chips)
        def _():
            wait_for(r.b_in.at[:, slot_rows(slot)], r.b_send.at[slot])

        @pl.when(chip >= k)
        def _():
            wait_for(r.g_out.at[:, slot_rows(slot)], r.g_send.at[slot])


def write_out(*refs):
    sources, results, sems = refs[:5], refs[5:10], refs[10]
    copies = [
        pltpu.make_async_copy(s, o, sems.at[i]) for i, (s, o) in enumerate(zip(sources, results))
    ]
    for copy in copies:
        copy.start()
    for copy in copies:
        copy.wait()


def dims(n_ctx, span, lanes, half, per):
    width = 2 * half
    window = min(8, n_ctx // 2 - 1)
    order = tuple(sorted(range(1, window + 1), key=lambda k: (k != window, (4, 1, 3, 2, 5, 7, 6, 8).index(k))))
    near = (window + 1) // 2
    raws = span // BLOCK
    return types.SimpleNamespace(
        n_ctx=n_ctx,
        span=span,
        lanes=lanes,
        half=half,
        per=per,
        width=width,
        heads=lanes // width,
        window=window,
        nb=window * per,
        order=order,
        groups=((0, near), (near, window)),
        raws=raws,
        parts=raws + 4,
        factors=3 * (raws + 4),
        delta=4 * (raws + 4),
        scale=width ** (-0.5),
        factor=width ** (-0.5) * LOG2E,
    )


def scratch(d):
    vmem = pltpu.VMEM
    dma = pltpu.SemaphoreType.DMA
    return dict(
        q=vmem((d.span, d.lanes), BF16),
        do=vmem((d.span, d.lanes), BF16),
        bkhalf=vmem((d.per, d.half), BF16),
        bvhalf=vmem((d.per, d.half), BF16),
        turn=vmem((d.span,), jnp.int32),
        chat=pltpu.SMEM((d.n_ctx,), jnp.int32),
        qt=vmem((d.heads, d.width, d.span), BF16),
        dot_t=vmem((d.heads, d.width, d.span), BF16),
        bias=vmem((d.span, d.span), F32),
        kv=vmem((2, d.width, d.span), BF16),
        kt=vmem((d.span, d.width), BF16),
        vt=vmem((d.span, d.width), BF16),
        beacon_out=vmem((d.per, d.width), BF16),
        b_in=vmem((2, d.nb, d.width), BF16),
        b_sib=vmem((2, d.nb, d.width), BF16),
        bkv=vmem((2 * d.nb, 2 * d.width), BF16),
        bkey=vmem((d.width, 2 * d.nb), BF16),
        e_raw=vmem((d.heads, d.span, d.span), F32),
        e_b=vmem((d.heads, 2 * d.nb, d.span), F32),
        dp_raw=vmem((d.heads, d.span, d.span), F32),
        dp_b=vmem((d.heads, 2 * d.nb, d.span), F32),
        s_raw=vmem((d.heads, d.span, d.span), BF16),
        s_b=vmem((d.heads, 2 * d.nb, d.span), BF16),
        stats=vmem((d.heads, 8 * (d.parts // 2 + 1), d.span), F32),
        gkt=vmem((d.width, d.span), F32),
        gvt=vmem((d.width, d.span), F32),
        gout=vmem((2, d.half, d.span), BF16),
        gin=vmem((2, d.half, d.span), BF16),
        x_out=vmem((d.nb, 2 * d.width), BF16),
        x_in=vmem((d.nb, 2 * d.width), BF16),
        own_out=vmem((2, d.per, d.width), BF16),
        g_own=vmem((d.nb, 2 * d.width), F32),
        g_out=vmem((2, d.nb, d.width), BF16),
        red=vmem((2, d.nb + d.per, d.width), BF16),
        load_sem=dma((8,)),
        pair_send=dma((2 * d.raws + 1,)),
        pair_recv=dma((2 * d.raws + 1,)),
        core_send=dma((6,)),
        core_recv=dma((6,)),
        own_send=dma((2,)),
        own_recv=dma,
        back_send=dma((2,)),
        back_recv=dma,
        b_send=dma((d.window,)),
        b_recv=dma((d.window,)),
        g_send=dma((d.window,)),
        g_recv=dma((d.window,)),
    )


IN_NAMES = ("chat_hbm", "q_hbm", "do_hbm", "k_hbm", "v_hbm", "bk_hbm", "bv_hbm", "turn_hbm")
OUT_NAMES = ("gq", "gk", "gv", "gbk", "gbv")


def on_device(
    n_ctx, query, grad_out, key_raw, value_raw, beacon_key, beacon_value, chat_of_span, turn_begin
):
    span, lanes = query.shape
    half, per = beacon_key.shape
    d = dims(n_ctx, span, lanes, half, per)
    space = scratch(d)
    hbm = pl.BlockSpec(memory_space=pltpu.HBM)
    vmem = pl.BlockSpec(memory_space=pltpu.VMEM)
    shapes = (
        jax.ShapeDtypeStruct((span, lanes), BF16),
        jax.ShapeDtypeStruct((half, span), F32),
        jax.ShapeDtypeStruct((half, span), F32),
        jax.ShapeDtypeStruct((per, half), F32),
        jax.ShapeDtypeStruct((per, half), F32),
    )
    operands = (
        chat_of_span,
        query,
        grad_out,
        key_raw,
        value_raw,
        beacon_key.T,
        beacon_value.T,
        turn_begin,
    )
    results = pl.pallas_call(
        functools.partial(kernel, IN_NAMES + OUT_NAMES + tuple(space), d),
        out_shape=shapes,
        in_specs=[hbm] * 8,
        out_specs=[vmem] * 5,
        scratch_shapes=list(space.values()),
        compiler_params=pltpu.CompilerParams(
            collective_id=0, has_side_effects=True, vmem_limit_bytes=48 * 1024 * 1024
        ),
        cost_estimate=pl.CostEstimate(
            flops=10 * d.heads * span * (span + 2 * d.nb) * d.width,
            bytes_accessed=6 * span * lanes,
            transcendentals=d.heads * span * (span + 2 * d.nb),
        ),
        name="beacon_backward",
    )(*[pltpu.with_memory_space_constraint(a, pltpu.HBM) for a in operands])
    results = pl.pallas_call(
        write_out,
        out_shape=shapes,
        in_specs=[vmem] * 5,
        out_specs=[hbm] * 5,
        scratch_shapes=[pltpu.SemaphoreType.DMA((5,))],
        compiler_params=pltpu.CompilerParams(vmem_limit_bytes=2 * 1024 * 1024),
        name="write_out",
    )(*results)
    return (*results[:3], results[3].T, results[4].T)


def solution(mesh):
    in_specs = (
        P("ctx", "group"),
        P("ctx", "group"),
        P("group", "ctx"),
        P("group", "ctx"),
        P("group", "ctx"),
        P("group", "ctx"),
        P(),
        P("ctx"),
    )
    out_specs = (
        P("ctx", "group"),
        P("group", "ctx"),
        P("group", "ctx"),
        P("group", "ctx"),
        P("group", "ctx"),
    )
    return jax.shard_map(
        functools.partial(on_device, mesh.shape["ctx"]),
        mesh=mesh,
        in_specs=in_specs,
        out_specs=out_specs,
        check_vma=False,
    )
```

```python
import functools
import math
import types

import jax
import jax.numpy as jnp
from jax import lax
from jax.experimental import pallas as pl
from jax.experimental.pallas import tpu as pltpu
from jax.sharding import PartitionSpec as P

MESH = pl.DeviceIdType.MESH
F32 = jnp.float32
BF16 = jnp.bfloat16
HIDDEN = -1e30
BLOCK = 128
LOG2E = math.log2(math.e)


def dot(a, b):
    return lax.dot_general(a, b, (((1,), (0,)), ((), ())), preferred_element_type=F32)


def head_lanes(h, width):
    return slice(h * width, (h + 1) * width)


def turn_queries(r, d):
    for h in range(d.heads):
        r.qt[h] = r.q[:, head_lanes(h, d.width)].T
        r.dot_t[h] = r.do[:, head_lanes(h, d.width)].T


def hide_tokens(r, d):
    begin = r.turn[...].reshape(1, d.span)
    rows = lax.broadcasted_iota(jnp.int32, (BLOCK, d.span), 0)
    cols = lax.broadcasted_iota(jnp.int32, (BLOCK, d.span), 1)
    for lo in range(0, d.span, BLOCK):
        at = rows + lo
        seen = (at <= cols) & (at >= begin)
        r.bias[lo : lo + BLOCK, :] = jnp.where(seen, 0.0, HIDDEN)


def note(r, h, part, lo, top, e, g):
    rows = (top, jnp.sum(e, axis=0, keepdims=True), jnp.sum(e * g, axis=0, keepdims=True))
    for i, row in enumerate(rows):
        r.stats[h, 3 * part + i : 3 * part + i + 1, lo:] = row
        if lo:
            fill = jnp.full((1, lo), HIDDEN if i == 0 else 0.0, F32)
            r.stats[h, 3 * part + i : 3 * part + i + 1, :lo] = fill


def raw_part(r, d, h, part):
    lo, hi = part * BLOCK, (part + 1) * BLOCK
    s = dot(r.kt[lo:hi, :], r.qt[h, :, lo:]) * d.factor + r.bias[lo:hi, lo:]
    r.e_raw[h, lo:hi, lo:] = s
    top = jnp.max(s, axis=0, keepdims=True)
    e = jnp.exp2(r.e_raw[h, lo:hi, lo:] - top)
    r.e_raw[h, lo:hi, lo:] = e
    g = dot(r.vt[lo:hi, :], r.dot_t[h, :, lo:])
    r.dp_raw[h, lo:hi, lo:] = g
    note(r, h, part, lo, top, e, g)


def slot_shift(r, d, me, side, slot):
    core = lax.rem(me, 2)
    k = d.order[slot]
    if side == 0:
        span_id = me - 2 * k
    elif k < d.window:
        span_id = me + 1 - 2 * core - 2 * k
    else:
        span_id = me - core + (1 - core) * (1 - 2 * k)
    shown = (span_id >= 0) & (r.chat[jnp.maximum(span_id, 0)] == r.chat[me])
    return jnp.where(shown, 0.0, HIDDEN).astype(F32)


def part_of(d, side, group):
    first, end = d.groups[group]
    base = side * d.nb
    return d.raws + 2 * side + group, first, base + first * d.per, base + end * d.per


def beacon_part(r, d, h, side, group, shifts):
    part, _, lo, hi = part_of(d, side, group)
    top = jnp.full((1, d.span), HIDDEN, F32)
    s = dot(r.bkv[lo:hi, : d.width], r.qt[h]) * d.factor
    for i, shift in enumerate(shifts):
        moved = s[i * d.per : (i + 1) * d.per] + shift
        r.e_b[h, lo + i * d.per : lo + (i + 1) * d.per, :] = moved
        top = jnp.maximum(top, jnp.max(moved, axis=0, keepdims=True))
    e = jnp.exp2(r.e_b[h, lo:hi, :] - top)
    r.e_b[h, lo:hi, :] = e
    g = dot(r.bkv[lo:hi, d.width :], r.dot_t[h])
    r.dp_b[h, lo:hi, :] = g
    note(r, h, part, 0, top, e, g)


def combine(r, d, h):
    tops = [r.stats[h, 3 * i : 3 * i + 1, :] for i in range(d.parts)]
    top = functools.reduce(jnp.maximum, tops)
    factors = [jnp.exp2(t - top) for t in tops]
    total = jnp.zeros((1, d.span), F32)
    delta = jnp.zeros((1, d.span), F32)
    for i, f in enumerate(factors):
        total = total + f * r.stats[h, 3 * i + 1 : 3 * i + 2, :]
        delta = delta + f * r.stats[h, 3 * i + 2 : 3 * i + 3, :]
    inv = 1.0 / total
    for i, f in enumerate(factors):
        r.stats[h, d.factors + i : d.factors + i + 1, :] = f * inv
    r.stats[h, d.delta : d.delta + 1, :] = delta * inv


def beacon_grads(r, d, side, group):
    part, _, lo, hi = part_of(d, side, group)
    gk = jnp.zeros((hi - lo, d.width), F32)
    gv = jnp.zeros((hi - lo, d.width), F32)
    for h in range(d.heads):
        p = r.e_b[h, lo:hi, :] * r.stats[h, d.factors + part : d.factors + part + 1, :]
        s = (p * (r.dp_b[h, lo:hi, :] - r.stats[h, d.delta : d.delta + 1, :])).astype(BF16)
        r.s_b[h, lo:hi, :] = s
        gk = gk + dot(s, r.q[:, head_lanes(h, d.width)])
        gv = gv + dot(p.astype(BF16), r.do[:, head_lanes(h, d.width)])
    return gk * d.scale, gv


def pack_halves(ref, at, gk, gv, half):
    ref[0, at, :] = jnp.concatenate([gk[:, :half], gv[:, :half]], axis=1).astype(BF16)
    ref[1, at, :] = jnp.concatenate([gk[:, half:], gv[:, half:]], axis=1).astype(BF16)


def raw_grads(r, d, lo):
    hi = lo + BLOCK
    at = d.factors + lo // BLOCK
    gk = jnp.zeros((BLOCK, d.width), F32)
    gv = jnp.zeros((BLOCK, d.width), F32)
    for h in range(d.heads):
        p = r.e_raw[h, lo:hi, lo:] * r.stats[h, at : at + 1, lo:]
        s = (p * (r.dp_raw[h, lo:hi, lo:] - r.stats[h, d.delta : d.delta + 1, lo:])).astype(BF16)
        r.s_raw[h, lo:hi, lo:] = s
        if lo % (2 * BLOCK):
            r.s_raw[h, lo:hi, lo - BLOCK : lo] = jnp.zeros((BLOCK, BLOCK), BF16)
        gk = gk + dot(s, r.q[lo:, head_lanes(h, d.width)])
        gv = gv + dot(p.astype(BF16), r.do[lo:, head_lanes(h, d.width)])
    r.gkt[:, lo:hi] = (gk * d.scale).T
    r.gvt[:, lo:hi] = gv.T


def query_grads(r, d, h):
    for lo in range(0, d.span, 2 * BLOCK):
        hi = lo + 2 * BLOCK
        g = dot(r.kv[0, :, :hi], r.s_raw[h, :hi, lo:hi]) + dot(r.bkey[...], r.s_b[h, :, lo:hi])
        r.gq[lo:hi, head_lanes(h, d.width)] = (g * d.scale).T.astype(BF16)


def unfold(r, d, side, group, halves):
    _, _, lo, hi = part_of(d, side, group)
    at = slice(lo - side * d.nb, hi - side * d.nb)
    low, high = halves[0, at, :], halves[1, at, :]
    half = d.half
    r.bkv[lo:hi, :] = jnp.concatenate(
        [low[:, :half], high[:, :half], low[:, half:], high[:, half:]], axis=1
    )


def wait_for(ref, sem):
    pltpu.make_async_copy(ref, ref, sem).wait()


def kernel(names, d, *refs):
    r = types.SimpleNamespace(**dict(zip(names, refs)))
    per, half, window, n_ctx = d.per, d.half, d.window, d.n_ctx

    z = lax.axis_index("group")
    me = lax.axis_index("ctx")
    parity = lax.rem(z, 2)
    even = z - parity
    partner = z + 1 - 2 * parity
    core = lax.rem(me, 2)
    sibling = me + 1 - 2 * core
    chip = lax.div(me, 2)
    chips = n_ctx // 2
    my_rows = pl.ds(parity * half, half)
    their_rows = pl.ds((1 - parity) * half, half)
    near = pl.ds(0, d.groups[0][1] * per)
    far = pl.ds(d.groups[0][1] * per, (window - d.groups[0][1]) * per)
    first = pl.ds(0, per)
    shared = pl.ds(per, (d.groups[0][1] - 1) * per)
    beyond = pl.ds(window * per, per)

    loads = [
        pltpu.make_async_copy(src, dst, r.load_sem.at[i])
        for i, (src, dst) in enumerate(
            (
                (r.bk_hbm, r.bkhalf),
                (r.bv_hbm, r.bvhalf),
                (r.k_hbm, r.kv.at[0, my_rows]),
                (r.v_hbm, r.kv.at[1, my_rows]),
                (r.q_hbm, r.q),
                (r.do_hbm, r.do),
                (r.turn_hbm, r.turn),
                (r.chat_hbm, r.chat),
            )
        )
    ]
    for copy in loads[:2]:
        copy.start()

    barrier = pltpu.get_barrier_semaphore()

    def greet(group, ctx):
        pl.semaphore_signal(barrier, inc=1, device_id=(group, ctx), device_id_type=MESH)

    for k in reversed(d.order):

        @pl.when(chip >= k)
        def _():
            for p in range(2):
                greet(even + p, me - 2 * k)

    greet(partner, me)
    greet(z, sibling)
    greet(partner, sibling)

    for copy in loads[2:]:
        copy.start()

    loads[0].wait()
    loads[1].wait()
    r.beacon_out[...] = jnp.concatenate([r.bkhalf[...], r.bvhalf[...]], axis=1)
    pl.semaphore_wait(barrier, 2 * jnp.minimum(window, chips - 1 - chip) + 3)

    def remote(src, dst, send, recv, group, ctx):
        return pltpu.make_async_remote_copy(
            src_ref=src,
            dst_ref=dst,
            send_sem=send,
            recv_sem=recv,
            device_id=(group, ctx),
            device_id_type=MESH,
        )

    def to_partner(i, src, dst):
        return remote(src, dst, r.pair_send.at[i], r.pair_recv.at[i], partner, me)

    def to_sibling(i, src, dst):
        return remote(src, dst, r.core_send.at[i], r.core_recv.at[i], z, sibling)

    raw_blocks = range(0, d.span, BLOCK)
    pair = []
    pair_back = []
    mine = r.kv.at[:, my_rows]
    pair.append(to_partner(2 * d.raws, mine, mine))
    for i, lo in enumerate(raw_blocks):
        at = pl.ds(lo, BLOCK)
        pair_back.append(to_partner(d.raws + i, r.gout.at[:, :, at], r.gin.at[:, :, at]))
    cores = [
        to_sibling(0, r.b_in.at[:, shared], r.b_sib.at[:, shared]),
        to_sibling(1, r.b_in.at[:, first], r.b_sib.at[:, first]),
        to_sibling(2, r.b_in.at[:, far], r.b_sib.at[:, far]),
        to_sibling(3, r.x_out.at[far], r.x_in.at[far]),
        to_sibling(4, r.x_out.at[shared], r.x_in.at[shared]),
        to_sibling(5, r.x_out.at[first], r.x_in.at[first]),
    ]


    def push(group):
        for slot in reversed(range(*d.groups[group])):
            k = d.order[slot]

            @pl.when(chip + k < chips)
            def _():
                for p in range(2):
                    remote(
                        r.beacon_out,
                        r.b_in.at[parity, pl.ds(slot * per, per)],
                        r.b_send.at[slot],
                        r.b_recv.at[slot],
                        even + p,
                        me + 2 * k,
                    ).start()

    push(1)
    push(0)
    loads[2].wait()
    loads[3].wait()
    pair[0].start()

    own_chip = [
        remote(
            r.beacon_out,
            r.b_sib.at[parity, first],
            r.own_send.at[i],
            r.own_recv,
            group,
            sibling,
        )
        for i, group in enumerate((z, partner))
    ]

    @pl.when(core == 0)
    def _():
        for copy in own_chip:
            copy.start()

    for i in (4, 5, 6, 7):
        loads[i].wait()
    turn_queries(r, d)
    hide_tokens(r, d)

    @pl.when(core == 0)
    def _():
        r.x_in[first, :] = jnp.zeros((per, 2 * d.width), BF16)

    @pl.when(core == 1)
    def _():
        r.red[:, beyond, :] = jnp.zeros((2, per, d.width), BF16)

    nothing = jnp.zeros((2, per, d.width), BF16)
    for slot in range(window):
        k = d.order[slot]
        at = pl.ds(slot * per, per)

        @pl.when(chip < k)
        def _():
            r.b_in[:, at, :] = nothing

        @pl.when(chip + k >= chips)
        def _():
            r.red[:, at, :] = nothing


    def shifts(side, group):
        return [slot_shift(r, d, me, side, slot) for slot in range(*d.groups[group])]

    def attend(side, group, halves):
        unfold(r, d, side, group, halves)
        moves = shifts(side, group)
        for h in range(d.heads):
            beacon_part(r, d, h, side, group, moves)

    def raw(part):
        if part == 0:
            pair[0].wait_recv()
        lo, hi = part * BLOCK, (part + 1) * BLOCK
        r.kt[lo:hi, :] = r.kv[0, :, lo:hi].T
        r.vt[lo:hi, :] = r.kv[1, :, lo:hi].T
        for h in range(d.heads):
            raw_part(r, d, h, part)

    def slot_rows(slot):
        return pl.ds(slot * per, per)

    def arrived(group):
        for slot in range(*d.groups[group]):

            @pl.when(chip >= d.order[slot])
            def _():
                wait_for(r.b_in.at[:, slot_rows(slot)], r.b_recv.at[slot])

    def exchange_near():
        arrived(0)
        cores[0].start()

        @pl.when(core == 1)
        def _():
            cores[1].start()

    def exchange_far():
        arrived(1)
        cores[2].start()

    def near_from_sibling():
        cores[0].wait_recv()

        @pl.when(core == 0)
        def _():
            cores[1].wait_recv()

        @pl.when(core == 1)
        def _():
            wait_for(r.b_sib.at[:, first], r.own_recv)

        attend(1, 0, r.b_sib)

    exchange_near()
    attend(0, 0, r.b_in)
    exchange_far()
    attend(0, 1, r.b_in)
    near_from_sibling()
    raw(0)
    raw(1)
    cores[2].wait_recv()
    attend(1, 1, r.b_sib)
    raw(2)
    raw(3)
    for h in range(d.heads):
        combine(r, d, h)

    def to_other_core(group):
        _, _, lo, hi = part_of(d, 0, group)
        gk, gv = beacon_grads(r, d, 1, group)
        r.x_out[lo:hi, : d.width] = gk.astype(BF16)
        r.x_out[lo:hi, d.width :] = gv.astype(BF16)

    own_back = [
        remote(
            r.own_out.at[p],
            r.red.at[parity, beyond],
            r.back_send.at[p],
            r.back_recv,
            even + p,
            sibling,
        )
        for p in range(2)
    ]


    def to_owners(group):
        _, _, lo, hi = part_of(d, 0, group)
        gk = r.g_own[lo:hi, : d.width] + r.x_in[lo:hi, : d.width].astype(F32)
        gv = r.g_own[lo:hi, d.width :] + r.x_in[lo:hi, d.width :].astype(F32)
        pack_halves(r.g_out, slice(lo, hi), gk, gv, half)
        for slot in reversed(range(*d.groups[group])):
            k = d.order[slot]

            @pl.when(chip >= k)
            def _():
                at = pl.ds(slot * per, per)
                for p in range(2):
                    remote(
                        r.g_out.at[p, at],
                        r.red.at[parity, at],
                        r.g_send.at[slot],
                        r.g_recv.at[slot],
                        even + p,
                        me - 2 * k,
                    ).start()

    def raw_back(part):
        lo = part * BLOCK
        raw_grads(r, d, lo)
        r.gout[0, :, lo : lo + BLOCK] = r.gkt[their_rows, lo : lo + BLOCK].astype(BF16)
        r.gout[1, :, lo : lo + BLOCK] = r.gvt[their_rows, lo : lo + BLOCK].astype(BF16)
        pair_back[part].start()

    def far_to_sibling():
        to_other_core(1)
        cores[3].start()

    def near_to_sibling():
        to_other_core(0)
        cores[4].start()

        @pl.when(core == 0)
        def _():
            cores[5].start()

        own = r.x_out[first, :]
        pack_halves(r.own_out, slice(None), own[:, : d.width], own[:, d.width :], half)

        @pl.when(core == 1)
        def _():
            for copy in own_back:
                copy.start()

    def own_grads(group):
        _, _, lo, hi = part_of(d, 0, group)
        gk, gv = beacon_grads(r, d, 0, group)
        r.g_own[lo:hi, : d.width] = gk
        r.g_own[lo:hi, d.width :] = gv

    def far_to_owners():
        cores[3].wait_recv()
        to_owners(1)

    def near_to_owners():
        cores[4].wait_recv()

        @pl.when(core == 1)
        def _():
            cores[5].wait_recv()

        to_owners(0)

    far_to_sibling()
    own_grads(1)
    near_to_sibling()
    far_to_owners()
    raw_back(0)
    own_grads(0)
    near_to_owners()
    raw_back(1)
    raw_back(2)
    raw_back(3)

    r.bkey[...] = r.bkv[:, : d.width].T
    for h in range(d.heads):
        query_grads(r, d, h)

    for slot in range(window):

        @pl.when(chip + d.order[slot] < chips)
        def _():
            wait_for(r.red.at[:, slot_rows(slot)], r.g_recv.at[slot])


    @pl.when(core == 0)
    def _():
        wait_for(r.red.at[:, beyond], r.back_recv)

    total = jnp.zeros((per, d.width), F32)
    for p in range(2):
        for k in range(window + 1):
            total = total + r.red[p, k * per : (k + 1) * per, :].astype(F32)
    r.gbk[...] = total[:, :half]
    r.gbv[...] = total[:, half:]

    for copy in pair_back:
        copy.wait_recv()
    r.gk[...] = r.gkt[my_rows, :] + r.gin[0].astype(F32)
    r.gv[...] = r.gvt[my_rows, :] + r.gin[1].astype(F32)

    for copy in pair + pair_back:
        copy.wait_send()
    for i in (0, 2, 3, 4):
        cores[i].wait_send()

    @pl.when(core == 0)
    def _():
        cores[5].wait_send()
        for copy in own_chip:
            copy.wait_send()

    @pl.when(core == 1)
    def _():
        cores[1].wait_send()
        for copy in own_back:
            copy.wait_send()

    for slot in range(window):
        k = d.order[slot]

        @pl.when(chip + k < chips)
        def _():
            wait_for(r.b_in.at[:, slot_rows(slot)], r.b_send.at[slot])

        @pl.when(chip >= k)
        def _():
            wait_for(r.g_out.at[:, slot_rows(slot)], r.g_send.at[slot])


def write_out(*refs):
    sources, results, sems = refs[:5], refs[5:10], refs[10]
    copies = [
        pltpu.make_async_copy(s, o, sems.at[i]) for i, (s, o) in enumerate(zip(sources, results))
    ]
    for copy in copies:
        copy.start()
    for copy in copies:
        copy.wait()


def dims(n_ctx, span, lanes, half, per):
    width = 2 * half
    window = min(8, n_ctx // 2 - 1)
    order = tuple(sorted(range(1, window + 1), key=lambda k: (k != window, (4, 1, 3, 2, 5, 7, 6, 8).index(k))))
    near = (window + 1) // 2
    raws = span // BLOCK
    return types.SimpleNamespace(
        n_ctx=n_ctx,
        span=span,
        lanes=lanes,
        half=half,
        per=per,
        width=width,
        heads=lanes // width,
        window=window,
        nb=window * per,
        order=order,
        groups=((0, near), (near, window)),
        raws=raws,
        parts=raws + 4,
        factors=3 * (raws + 4),
        delta=4 * (raws + 4),
        scale=width ** (-0.5),
        factor=width ** (-0.5) * LOG2E,
    )


def scratch(d):
    vmem = pltpu.VMEM
    dma = pltpu.SemaphoreType.DMA
    return dict(
        q=vmem((d.span, d.lanes), BF16),
        do=vmem((d.span, d.lanes), BF16),
        bkhalf=vmem((d.per, d.half), BF16),
        bvhalf=vmem((d.per, d.half), BF16),
        turn=vmem((d.span,), jnp.int32),
        chat=pltpu.SMEM((d.n_ctx,), jnp.int32),
        qt=vmem((d.heads, d.width, d.span), BF16),
        dot_t=vmem((d.heads, d.width, d.span), BF16),
        bias=vmem((d.span, d.span), F32),
        kv=vmem((2, d.width, d.span), BF16),
        kt=vmem((d.span, d.width), BF16),
        vt=vmem((d.span, d.width), BF16),
        beacon_out=vmem((d.per, d.width), BF16),
        b_in=vmem((2, d.nb, d.width), BF16),
        b_sib=vmem((2, d.nb, d.width), BF16),
        bkv=vmem((2 * d.nb, 2 * d.width), BF16),
        bkey=vmem((d.width, 2 * d.nb), BF16),
        e_raw=vmem((d.heads, d.span, d.span), F32),
        e_b=vmem((d.heads, 2 * d.nb, d.span), F32),
        dp_raw=vmem((d.heads, d.span, d.span), F32),
        dp_b=vmem((d.heads, 2 * d.nb, d.span), F32),
        s_raw=vmem((d.heads, d.span, d.span), BF16),
        s_b=vmem((d.heads, 2 * d.nb, d.span), BF16),
        stats=vmem((d.heads, 8 * (d.parts // 2 + 1), d.span), F32),
        gkt=vmem((d.width, d.span), F32),
        gvt=vmem((d.width, d.span), F32),
        gout=vmem((2, d.half, d.span), BF16),
        gin=vmem((2, d.half, d.span), BF16),
        x_out=vmem((d.nb, 2 * d.width), BF16),
        x_in=vmem((d.nb, 2 * d.width), BF16),
        own_out=vmem((2, d.per, d.width), BF16),
        g_own=vmem((d.nb, 2 * d.width), F32),
        g_out=vmem((2, d.nb, d.width), BF16),
        red=vmem((2, d.nb + d.per, d.width), BF16),
        load_sem=dma((8,)),
        pair_send=dma((2 * d.raws + 1,)),
        pair_recv=dma((2 * d.raws + 1,)),
        core_send=dma((6,)),
        core_recv=dma((6,)),
        own_send=dma((2,)),
        own_recv=dma,
        back_send=dma((2,)),
        back_recv=dma,
        b_send=dma((d.window,)),
        b_recv=dma((d.window,)),
        g_send=dma((d.window,)),
        g_recv=dma((d.window,)),
    )


IN_NAMES = ("chat_hbm", "q_hbm", "do_hbm", "k_hbm", "v_hbm", "bk_hbm", "bv_hbm", "turn_hbm")
OUT_NAMES = ("gq", "gk", "gv", "gbk", "gbv")


def on_device(
    n_ctx, query, grad_out, key_raw, value_raw, beacon_key, beacon_value, chat_of_span, turn_begin
):
    span, lanes = query.shape
    half, per = beacon_key.shape
    d = dims(n_ctx, span, lanes, half, per)
    space = scratch(d)
    hbm = pl.BlockSpec(memory_space=pltpu.HBM)
    vmem = pl.BlockSpec(memory_space=pltpu.VMEM)
    shapes = (
        jax.ShapeDtypeStruct((span, lanes), BF16),
        jax.ShapeDtypeStruct((half, span), F32),
        jax.ShapeDtypeStruct((half, span), F32),
        jax.ShapeDtypeStruct((per, half), F32),
        jax.ShapeDtypeStruct((per, half), F32),
    )
    operands = (
        chat_of_span,
        query,
        grad_out,
        key_raw,
        value_raw,
        beacon_key.T,
        beacon_value.T,
        turn_begin,
    )
    results = pl.pallas_call(
        functools.partial(kernel, IN_NAMES + OUT_NAMES + tuple(space), d),
        out_shape=shapes,
        in_specs=[hbm] * 8,
        out_specs=[vmem] * 5,
        scratch_shapes=list(space.values()),
        compiler_params=pltpu.CompilerParams(
            collective_id=0, has_side_effects=True, vmem_limit_bytes=48 * 1024 * 1024
        ),
        cost_estimate=pl.CostEstimate(
            flops=10 * d.heads * span * (span + 2 * d.nb) * d.width,
            bytes_accessed=6 * span * lanes,
            transcendentals=d.heads * span * (span + 2 * d.nb),
        ),
        name="beacon_backward",
    )(*[pltpu.with_memory_space_constraint(a, pltpu.HBM) for a in operands])
    results = pl.pallas_call(
        write_out,
        out_shape=shapes,
        in_specs=[vmem] * 5,
        out_specs=[hbm] * 5,
        scratch_shapes=[pltpu.SemaphoreType.DMA((5,))],
        compiler_params=pltpu.CompilerParams(vmem_limit_bytes=2 * 1024 * 1024),
        name="write_out",
    )(*results)
    return (*results[:3], results[3].T, results[4].T)


def solution(mesh):
    in_specs = (
        P("ctx", "group"),
        P("ctx", "group"),
        P("group", "ctx"),
        P("group", "ctx"),
        P("group", "ctx"),
        P("group", "ctx"),
        P(),
        P("ctx"),
    )
    out_specs = (
        P("ctx", "group"),
        P("group", "ctx"),
        P("group", "ctx"),
        P("group", "ctx"),
        P("group", "ctx"),
    )
    return jax.shard_map(
        functools.partial(on_device, mesh.shape["ctx"]),
        mesh=mesh,
        in_specs=in_specs,
        out_specs=out_specs,
        check_vma=False,
    )
```

```python
import functools
import math
import types

import jax
import jax.numpy as jnp
from jax import lax
from jax.experimental import pallas as pl
from jax.experimental.pallas import tpu as pltpu
from jax.sharding import PartitionSpec as P

MESH = pl.DeviceIdType.MESH
F32 = jnp.float32
BF16 = jnp.bfloat16
HIDDEN = -1e30
BLOCK = 128
LOG2E = math.log2(math.e)


def dot(a, b):
    return lax.dot_general(a, b, (((1,), (0,)), ((), ())), preferred_element_type=F32)


def head_lanes(h, width):
    return slice(h * width, (h + 1) * width)


def turn_queries(r, d):
    for h in range(d.heads):
        r.qt[h] = r.q[:, head_lanes(h, d.width)].T
        r.dot_t[h] = r.do[:, head_lanes(h, d.width)].T


def hide_tokens(r, d):
    begin = r.turn[...].reshape(1, d.span)
    rows = lax.broadcasted_iota(jnp.int32, (BLOCK, d.span), 0)
    cols = lax.broadcasted_iota(jnp.int32, (BLOCK, d.span), 1)
    for lo in range(0, d.span, BLOCK):
        at = rows + lo
        seen = (at <= cols) & (at >= begin)
        r.bias[lo : lo + BLOCK, :] = jnp.where(seen, 0.0, HIDDEN)


def note(r, h, part, lo, top, e, g):
    rows = (top, jnp.sum(e, axis=0, keepdims=True), jnp.sum(e * g, axis=0, keepdims=True))
    for i, row in enumerate(rows):
        r.stats[h, 3 * part + i : 3 * part + i + 1, lo:] = row
        if lo:
            fill = jnp.full((1, lo), HIDDEN if i == 0 else 0.0, F32)
            r.stats[h, 3 * part + i : 3 * part + i + 1, :lo] = fill


def raw_part(r, d, h, part):
    lo, hi = part * BLOCK, (part + 1) * BLOCK
    s = dot(r.kt[lo:hi, :], r.qt[h, :, lo:]) * d.factor + r.bias[lo:hi, lo:]
    r.e_raw[h, lo:hi, lo:] = s
    top = jnp.max(s, axis=0, keepdims=True)
    e = jnp.exp2(r.e_raw[h, lo:hi, lo:] - top)
    r.e_raw[h, lo:hi, lo:] = e
    g = dot(r.vt[lo:hi, :], r.dot_t[h, :, lo:])
    r.dp_raw[h, lo:hi, lo:] = g
    note(r, h, part, lo, top, e, g)


def slot_shift(r, d, me, side, slot):
    core = lax.rem(me, 2)
    k = d.order[slot]
    if side == 0:
        span_id = me - 2 * k
    elif k < d.window:
        span_id = me + 1 - 2 * core - 2 * k
    else:
        span_id = me - core + (1 - core) * (1 - 2 * k)
    shown = (span_id >= 0) & (r.chat[jnp.maximum(span_id, 0)] == r.chat[me])
    return jnp.where(shown, 0.0, HIDDEN).astype(F32)


def part_of(d, side, group):
    first, end = d.groups[group]
    base = side * d.nb
    return d.raws + 2 * side + group, first, base + first * d.per, base + end * d.per


def beacon_part(r, d, h, side, group, shifts):
    part, _, lo, hi = part_of(d, side, group)
    top = jnp.full((1, d.span), HIDDEN, F32)
    s = dot(r.bkv[lo:hi, : d.width], r.qt[h]) * d.factor
    for i, shift in enumerate(shifts):
        moved = s[i * d.per : (i + 1) * d.per] + shift
        r.e_b[h, lo + i * d.per : lo + (i + 1) * d.per, :] = moved
        top = jnp.maximum(top, jnp.max(moved, axis=0, keepdims=True))
    e = jnp.exp2(r.e_b[h, lo:hi, :] - top)
    r.e_b[h, lo:hi, :] = e
    g = dot(r.bkv[lo:hi, d.width :], r.dot_t[h])
    r.dp_b[h, lo:hi, :] = g
    note(r, h, part, 0, top, e, g)


def combine(r, d, h):
    tops = [r.stats[h, 3 * i : 3 * i + 1, :] for i in range(d.parts)]
    top = functools.reduce(jnp.maximum, tops)
    factors = [jnp.exp2(t - top) for t in tops]
    total = jnp.zeros((1, d.span), F32)
    delta = jnp.zeros((1, d.span), F32)
    for i, f in enumerate(factors):
        total = total + f * r.stats[h, 3 * i + 1 : 3 * i + 2, :]
        delta = delta + f * r.stats[h, 3 * i + 2 : 3 * i + 3, :]
    inv = 1.0 / total
    for i, f in enumerate(factors):
        r.stats[h, d.factors + i : d.factors + i + 1, :] = f * inv
    r.stats[h, d.delta : d.delta + 1, :] = delta * inv


def beacon_grads(r, d, side, group):
    part, _, lo, hi = part_of(d, side, group)
    gk = jnp.zeros((hi - lo, d.width), F32)
    gv = jnp.zeros((hi - lo, d.width), F32)
    for h in range(d.heads):
        p = r.e_b[h, lo:hi, :] * r.stats[h, d.factors + part : d.factors + part + 1, :]
        s = (p * (r.dp_b[h, lo:hi, :] - r.stats[h, d.delta : d.delta + 1, :])).astype(BF16)
        r.s_b[h, lo:hi, :] = s
        gk = gk + dot(s, r.q[:, head_lanes(h, d.width)])
        gv = gv + dot(p.astype(BF16), r.do[:, head_lanes(h, d.width)])
    return gk * d.scale, gv


def pack_halves(ref, at, gk, gv, half):
    ref[0, at, :] = jnp.concatenate([gk[:, :half], gv[:, :half]], axis=1).astype(BF16)
    ref[1, at, :] = jnp.concatenate([gk[:, half:], gv[:, half:]], axis=1).astype(BF16)


def raw_grads(r, d, lo):
    hi = lo + BLOCK
    at = d.factors + lo // BLOCK
    gk = jnp.zeros((BLOCK, d.width), F32)
    gv = jnp.zeros((BLOCK, d.width), F32)
    for h in range(d.heads):
        p = r.e_raw[h, lo:hi, lo:] * r.stats[h, at : at + 1, lo:]
        s = (p * (r.dp_raw[h, lo:hi, lo:] - r.stats[h, d.delta : d.delta + 1, lo:])).astype(BF16)
        r.s_raw[h, lo:hi, lo:] = s
        if lo % (2 * BLOCK):
            r.s_raw[h, lo:hi, lo - BLOCK : lo] = jnp.zeros((BLOCK, BLOCK), BF16)
        gk = gk + dot(s, r.q[lo:, head_lanes(h, d.width)])
        gv = gv + dot(p.astype(BF16), r.do[lo:, head_lanes(h, d.width)])
    r.gkt[:, lo:hi] = (gk * d.scale).T
    r.gvt[:, lo:hi] = gv.T


def query_grads(r, d, h):
    for lo in range(0, d.span, 2 * BLOCK):
        hi = lo + 2 * BLOCK
        g = dot(r.kv[0, :, :hi], r.s_raw[h, :hi, lo:hi]) + dot(r.bkey[...], r.s_b[h, :, lo:hi])
        r.gq[lo:hi, head_lanes(h, d.width)] = (g * d.scale).T.astype(BF16)


def unfold(r, d, side, group, halves):
    _, _, lo, hi = part_of(d, side, group)
    at = slice(lo - side * d.nb, hi - side * d.nb)
    low, high = halves[0, at, :], halves[1, at, :]
    half = d.half
    r.bkv[lo:hi, :] = jnp.concatenate(
        [low[:, :half], high[:, :half], low[:, half:], high[:, half:]], axis=1
    )


def wait_for(ref, sem):
    pltpu.make_async_copy(ref, ref, sem).wait()


def kernel(names, d, *refs):
    r = types.SimpleNamespace(**dict(zip(names, refs)))
    per, half, window, n_ctx = d.per, d.half, d.window, d.n_ctx

    z = lax.axis_index("group")
    me = lax.axis_index("ctx")
    parity = lax.rem(z, 2)
    even = z - parity
    partner = z + 1 - 2 * parity
    core = lax.rem(me, 2)
    sibling = me + 1 - 2 * core
    chip = lax.div(me, 2)
    chips = n_ctx // 2
    my_rows = pl.ds(parity * half, half)
    their_rows = pl.ds((1 - parity) * half, half)
    near = pl.ds(0, d.groups[0][1] * per)
    far = pl.ds(d.groups[0][1] * per, (window - d.groups[0][1]) * per)
    first = pl.ds(0, per)
    shared = pl.ds(per, (d.groups[0][1] - 1) * per)
    beyond = pl.ds(window * per, per)

    loads = [
        pltpu.make_async_copy(src, dst, r.load_sem.at[i])
        for i, (src, dst) in enumerate(
            (
                (r.bk_hbm, r.bkhalf),
                (r.bv_hbm, r.bvhalf),
                (r.k_hbm, r.kv.at[0, my_rows]),
                (r.v_hbm, r.kv.at[1, my_rows]),
                (r.q_hbm, r.q),
                (r.do_hbm, r.do),
                (r.turn_hbm, r.turn),
                (r.chat_hbm, r.chat),
            )
        )
    ]
    for copy in loads[:2]:
        copy.start()

    barrier = pltpu.get_barrier_semaphore()

    def greet(group, ctx):
        pl.semaphore_signal(barrier, inc=1, device_id=(group, ctx), device_id_type=MESH)

    for k in reversed(d.order):

        @pl.when(chip >= k)
        def _():
            for p in range(2):
                greet(even + p, me - 2 * k)

    greet(partner, me)
    greet(z, sibling)
    greet(partner, sibling)

    for copy in loads[2:]:
        copy.start()

    loads[0].wait()
    loads[1].wait()
    r.beacon_out[...] = jnp.concatenate([r.bkhalf[...], r.bvhalf[...]], axis=1)
    pl.semaphore_wait(barrier, 2 * jnp.minimum(window, chips - 1 - chip) + 3)

    def remote(src, dst, send, recv, group, ctx):
        return pltpu.make_async_remote_copy(
            src_ref=src,
            dst_ref=dst,
            send_sem=send,
            recv_sem=recv,
            device_id=(group, ctx),
            device_id_type=MESH,
        )

    def to_partner(i, src, dst):
        return remote(src, dst, r.pair_send.at[i], r.pair_recv.at[i], partner, me)

    def to_sibling(i, src, dst):
        return remote(src, dst, r.core_send.at[i], r.core_recv.at[i], z, sibling)

    raw_blocks = range(0, d.span, BLOCK)
    pair = []
    pair_back = []
    mine = r.kv.at[:, my_rows]
    pair.append(to_partner(2 * d.raws, mine, mine))
    for i, lo in enumerate(raw_blocks):
        at = pl.ds(lo, BLOCK)
        pair_back.append(to_partner(d.raws + i, r.gout.at[:, :, at], r.gin.at[:, :, at]))
    cores = [
        to_sibling(0, r.b_in.at[:, shared], r.b_sib.at[:, shared]),
        to_sibling(1, r.b_in.at[:, first], r.b_sib.at[:, first]),
        to_sibling(2, r.b_in.at[:, far], r.b_sib.at[:, far]),
        to_sibling(3, r.x_out.at[far], r.x_in.at[far]),
        to_sibling(4, r.x_out.at[shared], r.x_in.at[shared]),
        to_sibling(5, r.x_out.at[first], r.x_in.at[first]),
    ]


    def push(group):
        for slot in reversed(range(*d.groups[group])):
            k = d.order[slot]

            @pl.when(chip + k < chips)
            def _():
                for p in range(2):
                    remote(
                        r.beacon_out,
                        r.b_in.at[parity, pl.ds(slot * per, per)],
                        r.b_send.at[slot],
                        r.b_recv.at[slot],
                        even + p,
                        me + 2 * k,
                    ).start()

    push(1)
    push(0)
    loads[2].wait()
    loads[3].wait()
    pair[0].start()

    own_chip = [
        remote(
            r.beacon_out,
            r.b_sib.at[parity, first],
            r.own_send.at[i],
            r.own_recv,
            group,
            sibling,
        )
        for i, group in enumerate((z, partner))
    ]

    @pl.when(core == 0)
    def _():
        for copy in own_chip:
            copy.start()

    for i in (4, 5, 6, 7):
        loads[i].wait()
    turn_queries(r, d)
    hide_tokens(r, d)

    @pl.when(core == 0)
    def _():
        r.x_in[first, :] = jnp.zeros((per, 2 * d.width), BF16)

    @pl.when(core == 1)
    def _():
        r.red[:, beyond, :] = jnp.zeros((2, per, d.width), BF16)

    nothing = jnp.zeros((2, per, d.width), BF16)
    for slot in range(window):
        k = d.order[slot]
        at = pl.ds(slot * per, per)

        @pl.when(chip < k)
        def _():
            r.b_in[:, at, :] = nothing

        @pl.when(chip + k >= chips)
        def _():
            r.red[:, at, :] = nothing


    def shifts(side, group):
        return [slot_shift(r, d, me, side, slot) for slot in range(*d.groups[group])]

    def attend(side, group, halves):
        unfold(r, d, side, group, halves)
        moves = shifts(side, group)
        for h in range(d.heads):
            beacon_part(r, d, h, side, group, moves)

    def raw(part):
        if part == 0:
            pair[0].wait_recv()
        lo, hi = part * BLOCK, (part + 1) * BLOCK
        r.kt[lo:hi, :] = r.kv[0, :, lo:hi].T
        r.vt[lo:hi, :] = r.kv[1, :, lo:hi].T
        for h in range(d.heads):
            raw_part(r, d, h, part)

    def slot_rows(slot):
        return pl.ds(slot * per, per)

    def arrived(group):
        for slot in range(*d.groups[group]):

            @pl.when(chip >= d.order[slot])
            def _():
                wait_for(r.b_in.at[:, slot_rows(slot)], r.b_recv.at[slot])

    def exchange_near():
        arrived(0)
        cores[0].start()

        @pl.when(core == 1)
        def _():
            cores[1].start()

    def exchange_far():
        arrived(1)
        cores[2].start()

    def near_from_sibling():
        cores[0].wait_recv()

        @pl.when(core == 0)
        def _():
            cores[1].wait_recv()

        @pl.when(core == 1)
        def _():
            wait_for(r.b_sib.at[:, first], r.own_recv)

        attend(1, 0, r.b_sib)

    exchange_near()
    attend(0, 0, r.b_in)
    exchange_far()
    attend(0, 1, r.b_in)
    near_from_sibling()
    raw(0)
    raw(1)
    raw(2)
    raw(3)
    cores[2].wait_recv()
    attend(1, 1, r.b_sib)
    for h in range(d.heads):
        combine(r, d, h)

    def to_other_core(group):
        _, _, lo, hi = part_of(d, 0, group)
        gk, gv = beacon_grads(r, d, 1, group)
        r.x_out[lo:hi, : d.width] = gk.astype(BF16)
        r.x_out[lo:hi, d.width :] = gv.astype(BF16)

    own_back = [
        remote(
            r.own_out.at[p],
            r.red.at[parity, beyond],
            r.back_send.at[p],
            r.back_recv,
            even + p,
            sibling,
        )
        for p in range(2)
    ]


    def to_owners(group):
        _, _, lo, hi = part_of(d, 0, group)
        gk = r.g_own[lo:hi, : d.width] + r.x_in[lo:hi, : d.width].astype(F32)
        gv = r.g_own[lo:hi, d.width :] + r.x_in[lo:hi, d.width :].astype(F32)
        pack_halves(r.g_out, slice(lo, hi), gk, gv, half)
        for slot in reversed(range(*d.groups[group])):
            k = d.order[slot]

            @pl.when(chip >= k)
            def _():
                at = pl.ds(slot * per, per)
                for p in range(2):
                    remote(
                        r.g_out.at[p, at],
                        r.red.at[parity, at],
                        r.g_send.at[slot],
                        r.g_recv.at[slot],
                        even + p,
                        me - 2 * k,
                    ).start()

    def raw_back(part):
        lo = part * BLOCK
        raw_grads(r, d, lo)
        r.gout[0, :, lo : lo + BLOCK] = r.gkt[their_rows, lo : lo + BLOCK].astype(BF16)
        r.gout[1, :, lo : lo + BLOCK] = r.gvt[their_rows, lo : lo + BLOCK].astype(BF16)
        pair_back[part].start()

    def far_to_sibling():
        to_other_core(1)
        cores[3].start()

    def near_to_sibling():
        to_other_core(0)
        cores[4].start()

        @pl.when(core == 0)
        def _():
            cores[5].start()

        own = r.x_out[first, :]
        pack_halves(r.own_out, slice(None), own[:, : d.width], own[:, d.width :], half)

        @pl.when(core == 1)
        def _():
            for copy in own_back:
                copy.start()

    def own_grads(group):
        _, _, lo, hi = part_of(d, 0, group)
        gk, gv = beacon_grads(r, d, 0, group)
        r.g_own[lo:hi, : d.width] = gk
        r.g_own[lo:hi, d.width :] = gv

    def far_to_owners():
        cores[3].wait_recv()
        to_owners(1)

    def near_to_owners():
        cores[4].wait_recv()

        @pl.when(core == 1)
        def _():
            cores[5].wait_recv()

        to_owners(0)

    far_to_sibling()
    own_grads(1)
    near_to_sibling()
    far_to_owners()
    raw_back(0)
    own_grads(0)
    near_to_owners()
    raw_back(1)
    raw_back(2)
    raw_back(3)

    r.bkey[...] = r.bkv[:, : d.width].T
    for h in range(d.heads):
        query_grads(r, d, h)

    for slot in range(window):

        @pl.when(chip + d.order[slot] < chips)
        def _():
            wait_for(r.red.at[:, slot_rows(slot)], r.g_recv.at[slot])


    @pl.when(core == 0)
    def _():
        wait_for(r.red.at[:, beyond], r.back_recv)

    total = jnp.zeros((per, d.width), F32)
    for p in range(2):
        for k in range(window + 1):
            total = total + r.red[p, k * per : (k + 1) * per, :].astype(F32)
    r.gbk[...] = total[:, :half]
    r.gbv[...] = total[:, half:]

    for copy in pair_back:
        copy.wait_recv()
    r.gk[...] = r.gkt[my_rows, :] + r.gin[0].astype(F32)
    r.gv[...] = r.gvt[my_rows, :] + r.gin[1].astype(F32)

    for copy in pair + pair_back:
        copy.wait_send()
    for i in (0, 2, 3, 4):
        cores[i].wait_send()

    @pl.when(core == 0)
    def _():
        cores[5].wait_send()
        for copy in own_chip:
            copy.wait_send()

    @pl.when(core == 1)
    def _():
        cores[1].wait_send()
        for copy in own_back:
            copy.wait_send()

    for slot in range(window):
        k = d.order[slot]

        @pl.when(chip + k < chips)
        def _():
            wait_for(r.b_in.at[:, slot_rows(slot)], r.b_send.at[slot])

        @pl.when(chip >= k)
        def _():
            wait_for(r.g_out.at[:, slot_rows(slot)], r.g_send.at[slot])


def write_out(*refs):
    sources, results, sems = refs[:5], refs[5:10], refs[10]
    copies = [
        pltpu.make_async_copy(s, o, sems.at[i]) for i, (s, o) in enumerate(zip(sources, results))
    ]
    for copy in copies:
        copy.start()
    for copy in copies:
        copy.wait()


def dims(n_ctx, span, lanes, half, per):
    width = 2 * half
    window = min(8, n_ctx // 2 - 1)
    order = tuple(sorted(range(1, window + 1), key=lambda k: (k != window, (4, 1, 3, 2, 5, 7, 6, 8).index(k))))
    near = (window + 1) // 2
    raws = span // BLOCK
    return types.SimpleNamespace(
        n_ctx=n_ctx,
        span=span,
        lanes=lanes,
        half=half,
        per=per,
        width=width,
        heads=lanes // width,
        window=window,
        nb=window * per,
        order=order,
        groups=((0, near), (near, window)),
        raws=raws,
        parts=raws + 4,
        factors=3 * (raws + 4),
        delta=4 * (raws + 4),
        scale=width ** (-0.5),
        factor=width ** (-0.5) * LOG2E,
    )


def scratch(d):
    vmem = pltpu.VMEM
    dma = pltpu.SemaphoreType.DMA
    return dict(
        q=vmem((d.span, d.lanes), BF16),
        do=vmem((d.span, d.lanes), BF16),
        bkhalf=vmem((d.per, d.half), BF16),
        bvhalf=vmem((d.per, d.half), BF16),
        turn=vmem((d.span,), jnp.int32),
        chat=pltpu.SMEM((d.n_ctx,), jnp.int32),
        qt=vmem((d.heads, d.width, d.span), BF16),
        dot_t=vmem((d.heads, d.width, d.span), BF16),
        bias=vmem((d.span, d.span), F32),
        kv=vmem((2, d.width, d.span), BF16),
        kt=vmem((d.span, d.width), BF16),
        vt=vmem((d.span, d.width), BF16),
        beacon_out=vmem((d.per, d.width), BF16),
        b_in=vmem((2, d.nb, d.width), BF16),
        b_sib=vmem((2, d.nb, d.width), BF16),
        bkv=vmem((2 * d.nb, 2 * d.width), BF16),
        bkey=vmem((d.width, 2 * d.nb), BF16),
        e_raw=vmem((d.heads, d.span, d.span), F32),
        e_b=vmem((d.heads, 2 * d.nb, d.span), F32),
        dp_raw=vmem((d.heads, d.span, d.span), F32),
        dp_b=vmem((d.heads, 2 * d.nb, d.span), F32),
        s_raw=vmem((d.heads, d.span, d.span), BF16),
        s_b=vmem((d.heads, 2 * d.nb, d.span), BF16),
        stats=vmem((d.heads, 8 * (d.parts // 2 + 1), d.span), F32),
        gkt=vmem((d.width, d.span), F32),
        gvt=vmem((d.width, d.span), F32),
        gout=vmem((2, d.half, d.span), BF16),
        gin=vmem((2, d.half, d.span), BF16),
        x_out=vmem((d.nb, 2 * d.width), BF16),
        x_in=vmem((d.nb, 2 * d.width), BF16),
        own_out=vmem((2, d.per, d.width), BF16),
        g_own=vmem((d.nb, 2 * d.width), F32),
        g_out=vmem((2, d.nb, d.width), BF16),
        red=vmem((2, d.nb + d.per, d.width), BF16),
        load_sem=dma((8,)),
        pair_send=dma((2 * d.raws + 1,)),
        pair_recv=dma((2 * d.raws + 1,)),
        core_send=dma((6,)),
        core_recv=dma((6,)),
        own_send=dma((2,)),
        own_recv=dma,
        back_send=dma((2,)),
        back_recv=dma,
        b_send=dma((d.window,)),
        b_recv=dma((d.window,)),
        g_send=dma((d.window,)),
        g_recv=dma((d.window,)),
    )


IN_NAMES = ("chat_hbm", "q_hbm", "do_hbm", "k_hbm", "v_hbm", "bk_hbm", "bv_hbm", "turn_hbm")
OUT_NAMES = ("gq", "gk", "gv", "gbk", "gbv")


def on_device(
    n_ctx, query, grad_out, key_raw, value_raw, beacon_key, beacon_value, chat_of_span, turn_begin
):
    span, lanes = query.shape
    half, per = beacon_key.shape
    d = dims(n_ctx, span, lanes, half, per)
    space = scratch(d)
    hbm = pl.BlockSpec(memory_space=pltpu.HBM)
    vmem = pl.BlockSpec(memory_space=pltpu.VMEM)
    shapes = (
        jax.ShapeDtypeStruct((span, lanes), BF16),
        jax.ShapeDtypeStruct((half, span), F32),
        jax.ShapeDtypeStruct((half, span), F32),
        jax.ShapeDtypeStruct((per, half), F32),
        jax.ShapeDtypeStruct((per, half), F32),
    )
    operands = (
        chat_of_span,
        query,
        grad_out,
        key_raw,
        value_raw,
        beacon_key.T,
        beacon_value.T,
        turn_begin,
    )
    results = pl.pallas_call(
        functools.partial(kernel, IN_NAMES + OUT_NAMES + tuple(space), d),
        out_shape=shapes,
        in_specs=[hbm] * 8,
        out_specs=[vmem] * 5,
        scratch_shapes=list(space.values()),
        compiler_params=pltpu.CompilerParams(
            collective_id=0, has_side_effects=True, vmem_limit_bytes=48 * 1024 * 1024
        ),
        cost_estimate=pl.CostEstimate(
            flops=10 * d.heads * span * (span + 2 * d.nb) * d.width,
            bytes_accessed=6 * span * lanes,
            transcendentals=d.heads * span * (span + 2 * d.nb),
        ),
        name="beacon_backward",
    )(*[pltpu.with_memory_space_constraint(a, pltpu.HBM) for a in operands])
    results = pl.pallas_call(
        write_out,
        out_shape=shapes,
        in_specs=[vmem] * 5,
        out_specs=[hbm] * 5,
        scratch_shapes=[pltpu.SemaphoreType.DMA((5,))],
        compiler_params=pltpu.CompilerParams(vmem_limit_bytes=2 * 1024 * 1024),
        name="write_out",
    )(*results)
    return (*results[:3], results[3].T, results[4].T)


def solution(mesh):
    in_specs = (
        P("ctx", "group"),
        P("ctx", "group"),
        P("group", "ctx"),
        P("group", "ctx"),
        P("group", "ctx"),
        P("group", "ctx"),
        P(),
        P("ctx"),
    )
    out_specs = (
        P("ctx", "group"),
        P("group", "ctx"),
        P("group", "ctx"),
        P("group", "ctx"),
        P("group", "ctx"),
    )
    return jax.shard_map(
        functools.partial(on_device, mesh.shape["ctx"]),
        mesh=mesh,
        in_specs=in_specs,
        out_specs=out_specs,
        check_vma=False,
    )
```
